32 devices in a mesh: curve: 16 (over z, x, core), dp: 2 (over y).
Axes of the slice: x: 2, y: 2, z: 4, core: 2. Of those that a mesh axis runs over, the one named last changes fastest.
Arguments:
- points: bfloat16 [2, 8192, 512], P('dp', 'curve'), may hold values from -24 to 24
- grad_out: bfloat16 [2, 8192, 512], P('dp', 'curve'), may hold values from -6 to 6
- dest_dev: int32 [2, 8192], P('dp', 'curve'), may hold values from 0 to 15, as said below
- dest_row: int32 [2, 8192], P('dp', 'curve'), may hold values from 0 to 511
- w_qkv: bfloat16 [512, 1536], replicated, may hold values from -1 to 1
- w_out: bfloat16 [512, 512], replicated, may hold values from -0.25 to 0.25
Outputs:
- grad_points: bfloat16 [2, 8192, 512], P('dp', 'curve')
- grad_w_qkv: float32 [512, 1536], replicated
- grad_w_out: float32 [512, 512], replicated
The draws below stay inside these ranges and needn't reach their ends.
Inputs may be any that keep to these rules, and one draw needn't show every extreme that they name: `dest_dev`: together with dest_row it maps each group's scan points one to one onto the 8192 curve positions: every curve device of a group receives exactly 512 points, at most 64 of them from one scan device, and in every draw some scan device sends exactly 64 points to some curve device.
All inputs are finite; a program needn't handle non-finite values.
Results may differ from the reference program's by a relative error of at most 0.011.
The reference program's roundings to bfloat16 on the way count: a program that leaves them out, or rounds other values in their place, can miss the bound.
Values may be sent and summed in bfloat16 or wider, within the bound.
No kernel may reach another device: no remote copies, remote signals or barrier semaphores. Data moves between devices by JAX's collectives and lax.ppermute only.
A program may use at most 64 MiB of HBM per device.

```python
import math
import jax
import jax.numpy as jnp
from jax import lax

D = 512
HEADS = 8
PATCH = 512
SHIFT = 256
TOK_DEV = 512
POINTS = 8192
N_CURVE = 16
N_DP = 2


def route_tables(key):
    n_dev = N_CURVE
    per_dev = TOK_DEV
    mean_count = per_dev // n_dev

    def one_group(group_key):
        keys_list = jax.random.split(group_key, 5)
        spread = jax.random.randint(keys_list[0], (n_dev // 2,), 0, mean_count + 1)
        spread = spread.at[0].set(mean_count)
        pattern = jnp.stack([spread, -spread], axis=1).reshape(n_dev)
        counts = mean_count + jax.random.permutation(keys_list[1], pattern)
        upper = jnp.cumsum(counts).astype(jnp.int32)
        label = jax.random.permutation(keys_list[2], n_dev).astype(jnp.int32)
        unlabel = jnp.zeros((n_dev,), jnp.int32).at[label].set(jnp.arange(n_dev, dtype=jnp.int32))
        order_src = jax.vmap(lambda single: jax.random.permutation(single, per_dev))(jax.random.split(keys_list[3], n_dev)).astype(jnp.int32)
        order_dst = jax.vmap(lambda single: jax.random.permutation(single, per_dev))(jax.random.split(keys_list[4], n_dev)).astype(jnp.int32)
        offset = jnp.searchsorted(upper, order_src, side='right').astype(jnp.int32)
        sources = jnp.arange(n_dev, dtype=jnp.int32)[:, None]
        dest_label = (label[sources] + offset) % n_dev
        dest = unlabel[dest_label]
        rows_at = order_dst[dest, order_src]
        return (dest.reshape(-1), rows_at.reshape(-1))
    group_keys = jax.random.split(jax.random.fold_in(key, 4242), N_DP)
    return jax.vmap(one_group)(group_keys)


def draw_dest_dev(key, part):
    return route_tables(key)[0]


def draw_dest_row(key, part):
    return route_tables(key)[1]


def draw_points(key, part):
    first_key = jax.random.fold_in(jax.random.fold_in(key, 17), 0)
    shape = (N_DP, POINTS, D)
    return jnp.clip(jax.random.normal(first_key, shape, jnp.float32), -4.0, 4.0).astype(jnp.bfloat16)


def draw_w_qkv(key, part):
    first_key = jax.random.fold_in(jax.random.fold_in(key, 91), 0)
    sigma = D ** (-0.5)
    return (jnp.clip(jax.random.normal(first_key, (D, 3 * D), jnp.float32), -4.0, 4.0) * sigma).astype(jnp.bfloat16)


def levels(stream_key, dims, cuts, low, high):
    gain = 1.0
    for dim, parts in cuts:
        heights = jax.random.uniform(jax.random.fold_in(jax.random.fold_in(stream_key, 6), dim), (parts,), jnp.float32, low / len(cuts), high / len(cuts))
        gain = gain * jnp.repeat(jnp.exp(heights), dims[dim] // parts).reshape((-1,) + (1,) * (len(dims) - 1 - dim))
    return gain


def scatter_about(stream_key, shape, scale, reach, cuts=(), held_as=jnp.bfloat16):
    values = scale * jax.random.normal(stream_key, shape, jnp.float32)
    if cuts:
        values = values * levels(stream_key, shape, cuts, -0.22, 0.18)
    return jnp.clip(values, -reach, reach).astype(held_as)


def setup_inputs(seed: int = 0) -> dict:
    key_of = jax.random.split(jax.random.key(seed), 7)
    points = draw_points(jax.random.fold_in(key_of[6], 71), 0)
    grad_out = scatter_about(key_of[1], (N_DP, POINTS, D), 1.0, 6.0, ((0, 2), (1, 16)))
    dest_dev = draw_dest_dev(jax.random.fold_in(key_of[6], 71), 0)
    dest_row = draw_dest_row(jax.random.fold_in(key_of[6], 71), 0)
    w_qkv = draw_w_qkv(jax.random.fold_in(key_of[6], 71), 0)
    w_out = scatter_about(key_of[5], (D, D), D ** -0.5, 0.25)
    return {"points": points, "grad_out": grad_out, "dest_dev": dest_dev, "dest_row": dest_row, "w_qkv": w_qkv, "w_out": w_out}


def lowered(values):
    return lax.optimization_barrier(values.astype(jnp.bfloat16)).astype(jnp.float32)

def patch_backward(qkv_patch, grad_patch):
    head_dim = D // HEADS
    scale = 1.0 / math.sqrt(head_dim)
    queries = qkv_patch[:, :D].astype(jnp.float32).reshape(PATCH, HEADS, head_dim)
    keys_all = qkv_patch[:, D:2 * D].astype(jnp.float32).reshape(PATCH, HEADS, head_dim)
    values_all = qkv_patch[:, 2 * D:].astype(jnp.float32).reshape(PATCH, HEADS, head_dim)
    grads = grad_patch.astype(jnp.float32).reshape(PATCH, HEADS, head_dim)
    scores = jnp.einsum('qhd,khd->hqk', queries, keys_all) * scale
    probs = jax.nn.softmax(scores, axis=-1)
    probs_low = lowered(probs)
    attn = jnp.einsum('hqk,khd->qhd', probs_low, values_all).astype(jnp.bfloat16)
    delta = lax.optimization_barrier(jnp.sum(grads * attn.astype(jnp.float32), axis=-1))
    grad_values = jnp.einsum('hqk,qhd->khd', probs_low, grads)
    grad_probs = jnp.einsum('qhd,khd->hqk', grads, values_all)
    grad_scores = lowered(probs * (grad_probs - jnp.transpose(delta)[:, :, None]))
    grad_queries = jnp.einsum('hqk,khd->qhd', grad_scores, keys_all) * scale
    grad_keys = jnp.einsum('hqk,qhd->khd', grad_scores, queries) * scale
    grad_qkv = jnp.concatenate([grad_queries.reshape(PATCH, D), grad_keys.reshape(PATCH, D), grad_values.reshape(PATCH, D)], axis=1)
    return (attn.reshape(PATCH, D), grad_qkv.astype(jnp.bfloat16))

def reference(points, grad_out, dest_dev, dest_row, w_qkv, w_out):
    outputs = []
    weight_qkv = jnp.zeros((D, 3 * D), jnp.float32)
    weight_out = jnp.zeros((D, D), jnp.float32)
    for group in range(N_DP):
        position = (dest_dev[group].astype(jnp.int32) * TOK_DEV + dest_row[group].astype(jnp.int32)).astype(jnp.int32)
        curve_points = jnp.zeros((POINTS, D), jnp.bfloat16).at[position].set(points[group])
        curve_grads = jnp.zeros((POINTS, D), jnp.bfloat16).at[position].set(grad_out[group])
        rolled_points = jnp.roll(curve_points, -SHIFT, axis=0)
        rolled_grads = jnp.roll(curve_grads, -SHIFT, axis=0)
        qkv = jnp.dot(rolled_points, w_qkv, preferred_element_type=jnp.float32).astype(jnp.bfloat16)
        grad_attn = jnp.dot(rolled_grads, w_out.T, preferred_element_type=jnp.float32).astype(jnp.bfloat16)
        attn, grad_qkv = lax.map(lambda pair: patch_backward(pair[0], pair[1]), (qkv.reshape(POINTS // PATCH, PATCH, 3 * D), grad_attn.reshape(POINTS // PATCH, PATCH, D)))
        attn = attn.reshape(POINTS, D)
        grad_qkv = grad_qkv.reshape(POINTS, 3 * D)
        weight_qkv = weight_qkv + jnp.dot(rolled_points.T, grad_qkv, preferred_element_type=jnp.float32)
        weight_out = weight_out + jnp.dot(attn.T, rolled_grads, preferred_element_type=jnp.float32)
        input_grads = jnp.dot(grad_qkv, w_qkv.T, preferred_element_type=jnp.float32).astype(jnp.bfloat16)
        curve_input = jnp.roll(input_grads, SHIFT, axis=0)
        outputs.append(curve_input[position])
    return (jnp.stack(outputs), weight_qkv, weight_out)
```

```python
import math

import jax
import jax.numpy as jnp
from jax import lax
from jax.sharding import PartitionSpec as P

HEADS = 8
PATCH = 512


def from_behind(block, axis, distance):
    devices = range(lax.axis_size(axis))
    route = [((i - distance) % len(devices), i) for i in devices]
    return lax.ppermute(block, axis, route)


def contract(left, right, left_dim, right_dim):
    return lax.dot_general(
        left, right, (((left_dim,), (right_dim,)), ((), ())), preferred_element_type=jnp.float32
    )


def attend_backward(queries, keys_vals, grad_rows):
    width = queries.shape[1]
    head_dim = width // HEADS
    scale = 1.0 / math.sqrt(head_dim)
    attn_list, query_list, key_list, value_list = ([], [], [], [])
    for head in range(HEADS):
        lower = head * head_dim
        upper = lower + head_dim
        query_part = queries[:, lower:upper]
        key_part = keys_vals[:, lower:upper]
        value_part = keys_vals[:, width + lower : width + upper]
        grad_part = grad_rows[:, lower:upper]
        scores = contract(query_part, key_part, 1, 1) * scale
        probs = jax.nn.softmax(scores, axis=-1)
        probs_low = probs.astype(jnp.bfloat16)
        attn_part = jnp.dot(probs_low, value_part, preferred_element_type=jnp.float32).astype(
            jnp.bfloat16
        )
        delta = jnp.sum(
            grad_part.astype(jnp.float32) * attn_part.astype(jnp.float32), axis=1, keepdims=True
        )
        value_list.append(contract(probs_low, grad_part, 0, 0))
        grad_probs = contract(grad_part, value_part, 1, 1)
        grad_scores = (probs * (grad_probs - delta)).astype(jnp.bfloat16)
        query_list.append(
            jnp.dot(grad_scores, key_part, preferred_element_type=jnp.float32) * scale
        )
        key_list.append(contract(grad_scores, query_part, 0, 0) * scale)
        attn_list.append(attn_part)
    attn = jnp.concatenate(attn_list, axis=1)
    grad_queries = jnp.concatenate(query_list, axis=1)
    grad_kv = jnp.concatenate(key_list + value_list, axis=1)
    return (attn, grad_queries, grad_kv)


def finish(point_rows, grad_rows, attn, grad_qkv, w_qkv):
    input_grads = contract(grad_qkv, w_qkv, 1, 1).astype(jnp.bfloat16)
    part_qkv = contract(point_rows, grad_qkv, 0, 0)
    part_out = contract(attn, grad_rows, 0, 0)
    return (input_grads, part_qkv, part_out)


def work_patches(point_rows, grad_rows, w_qkv, w_out):
    width = w_out.shape[0]
    qkv = jnp.dot(point_rows, w_qkv, preferred_element_type=jnp.float32).astype(jnp.bfloat16)
    grad_attn = contract(grad_rows, w_out, 1, 1).astype(jnp.bfloat16)
    attn_list, grad_list = ([], [])
    upper = PATCH
    attn, grad_queries, grad_kv = attend_backward(
        qkv[0:upper, :width], qkv[0:upper, width:], grad_attn
    )
    attn_list.append(attn)
    grad_list.append(jnp.concatenate([grad_queries, grad_kv], axis=1))
    attn_all = attn_list[0]
    grad_qkv = grad_list[0].astype(jnp.bfloat16)
    return finish(point_rows, grad_rows, attn_all, grad_qkv, w_qkv)


def slot_table(home_dev, n_dev, capacity):
    rows = home_dev.shape[0]
    onehot = (home_dev[:, None] == jnp.arange(n_dev, dtype=jnp.int32)[None, :]).astype(jnp.bfloat16)
    row_ids = jnp.arange(rows, dtype=jnp.int32)
    lower_tri = (row_ids[:, None] >= row_ids[None, :]).astype(jnp.bfloat16)
    running = jnp.dot(lower_tri, onehot, preferred_element_type=jnp.float32)
    rank = jnp.sum(running * onehot.astype(jnp.float32), axis=1).astype(jnp.int32) - 1
    return home_dev * capacity + rank


def pack_rows(slots, home_row, point_rows, grad_rows, n_dev, capacity):
    rows, width = point_rows.shape
    total = n_dev * capacity
    send_points = (
        jnp.zeros((total, width), jnp.bfloat16)
        .at[slots]
        .set(point_rows)
        .reshape(n_dev, capacity, width)
    )
    send_grads = (
        jnp.zeros((total, width), jnp.bfloat16)
        .at[slots]
        .set(grad_rows)
        .reshape(n_dev, capacity, width)
    )
    send_rows = jnp.full((total,), rows, jnp.int32).at[slots].set(home_row).reshape(n_dev, capacity)
    return (send_points, send_grads, send_rows)


def place_rows(got_values, got_rows, rows):
    width = got_values.shape[-1]
    return (
        jnp.zeros((rows, width), jnp.bfloat16)
        .at[got_rows.reshape(-1)]
        .set(got_values.reshape(-1, width), mode="drop")
    )


def pick_rows(values, got_rows):
    rows, width = values.shape
    taken = jnp.take(values, jnp.minimum(got_rows.reshape(-1), rows - 1), axis=0)
    return taken.reshape(got_rows.shape[0], got_rows.shape[1], width)


def swap(block, axis, mask):
    size = lax.axis_size(axis)
    return lax.ppermute(block, axis, [(i, i ^ mask) for i in range(size)])


def split_rows(rows, side):
    half = rows.shape[0] // 2
    keep = lax.dynamic_slice_in_dim(rows, side * half, half, 0)
    send = lax.dynamic_slice_in_dim(rows, (1 - side) * half, half, 0)
    return (keep, send.astype(jnp.bfloat16))


def join_rows(own, got, side):
    return jnp.concatenate([jnp.where(side == 0, own, got), jnp.where(side == 0, got, own)], axis=0)


def order_blocks(blocks, place):
    count = blocks.shape[0]
    tail = blocks.shape[1:]
    bit = 1
    while bit < count:
        pairs = blocks.reshape(count // (2 * bit), 2, bit, *tail)
        blocks = jnp.where((place & bit) != 0, pairs[:, ::-1], pairs).reshape(count, *tail)
        bit *= 2
    return blocks


def sum_devices(total):
    me = lax.axis_index("curve")
    n_line = lax.axis_size("curve") // 4
    core, side_x, line, side_y = (me & 1, (me >> 1) & 1, me >> 2, lax.axis_index("dp"))
    keep, send = split_rows(total, core)
    part = keep + swap(send, "curve", 1).astype(jnp.float32)
    half = part.shape[0] // 2
    keep_a, send_a = split_rows(part[:half], side_x)
    keep_b, send_b = split_rows(part[half:], side_y)
    part_a = keep_a + swap(send_a, "curve", 2).astype(jnp.float32)
    part_b = keep_b + swap(send_b, "dp", 1).astype(jnp.float32)
    keep_a, send_a = split_rows(part_a, side_y)
    keep_b, send_b = split_rows(part_b, side_x)
    part_a = keep_a + swap(send_a, "dp", 1).astype(jnp.float32)
    part_b = keep_b + swap(send_b, "curve", 2).astype(jnp.float32)
    width = total.shape[1]
    rows = part_a.shape[0] // n_line
    both = jnp.stack([part_a.reshape(n_line, rows, width), part_b.reshape(n_line, rows, width)], axis=1)
    mine = lax.dynamic_index_in_dim(both, line, 0, keepdims=False)
    others = [
        swap(
            lax.dynamic_index_in_dim(both, line ^ k, 0, keepdims=False).astype(jnp.bfloat16),
            "curve",
            4 * k,
        )
        for k in range(1, n_line)
    ]
    for other in others:
        mine = mine + other.astype(jnp.float32)
    mine = mine.astype(jnp.bfloat16)
    blocks = jnp.stack([mine] + [swap(mine, "curve", 4 * k) for k in range(1, n_line)])
    blocks = order_blocks(blocks, line)
    full_a = blocks[:, 0].reshape(n_line * rows, width)
    full_b = blocks[:, 1].reshape(n_line * rows, width)
    got_a = swap(full_a, "dp", 1)
    got_b = swap(full_b, "curve", 2)
    full_a = join_rows(full_a, got_a, side_y)
    full_b = join_rows(full_b, got_b, side_x)
    got_a = swap(full_a, "curve", 2)
    got_b = swap(full_b, "dp", 1)
    half_rows = jnp.concatenate([join_rows(full_a, got_a, side_x), join_rows(full_b, got_b, side_y)])
    return join_rows(half_rows, swap(half_rows, "curve", 1), core).astype(jnp.float32)


def on_device(points, grad_out, dest_dev, dest_row, w_qkv, w_out):
    point_rows = points[0]
    grad_rows = grad_out[0]
    device_of = dest_dev[0]
    row_of = dest_row[0]
    rows, width = point_rows.shape
    n_dev = lax.axis_size("curve")
    capacity = 2 * rows // n_dev
    shift_rows = PATCH // 2
    slots = slot_table(device_of, n_dev, capacity)
    send_points, send_grads, send_rows = pack_rows(
        slots, row_of, point_rows, grad_rows, n_dev, capacity
    )
    got_points, got_grads, got_rows = (
        lax.all_to_all(send_points, "curve", split_axis=0, concat_axis=0, tiled=True),
        lax.all_to_all(send_grads, "curve", split_axis=0, concat_axis=0, tiled=True),
        lax.all_to_all(send_rows, "curve", split_axis=0, concat_axis=0, tiled=True),
    )
    own_points = place_rows(got_points, got_rows, rows)
    own_grads = place_rows(got_grads, got_rows, rows)
    head_pair = jnp.stack([own_points[:shift_rows], own_grads[:shift_rows]])
    following = from_behind(head_pair, "curve", -1)
    work_points = jnp.concatenate([own_points[shift_rows:], following[0]], axis=0)
    work_grads = jnp.concatenate([own_grads[shift_rows:], following[1]], axis=0)
    work_input, part_qkv, part_out = work_patches(work_points, work_grads, w_qkv, w_out)
    earlier = from_behind(work_input[rows - shift_rows :], "curve", 1)
    own_input = jnp.concatenate([earlier, work_input[: rows - shift_rows]], axis=0)
    returned = lax.all_to_all(
        pick_rows(own_input, got_rows), "curve", split_axis=0, concat_axis=0, tiled=True
    )
    result_rows = returned.reshape(n_dev * capacity, width)[slots]
    weights = sum_devices(jnp.concatenate([part_qkv, part_out], axis=1))
    n_qkv = part_qkv.shape[1]
    return (result_rows[None], weights[:, :n_qkv], weights[:, n_qkv:])


def solution(mesh):
    placed = (
        P("dp", "curve", None),
        P("dp", "curve", None),
        P("dp", "curve"),
        P("dp", "curve"),
        P(),
        P(),
    )
    return jax.shard_map(
        on_device,
        mesh=mesh,
        in_specs=placed,
        out_specs=(P("dp", "curve", None), P(), P()),
        check_vma=False,
    )
```

```python
import functools
import math

import jax
import jax.numpy as jnp
from jax import lax
from jax.experimental import pallas as pl
from jax.experimental.pallas import tpu as pltpu
from jax.sharding import PartitionSpec as P

HEADS = 8
PATCH = 512
INFO_ROWS = 8
LANES = 128


def from_behind(block, axis, distance):
    devices = range(lax.axis_size(axis))
    route = [((i - distance) % len(devices), i) for i in devices]
    return lax.ppermute(block, axis, route)


def contract(left, right, left_dim, right_dim):
    return lax.dot_general(
        left, right, (((left_dim,), (right_dim,)), ((), ())), preferred_element_type=jnp.float32
    )


def iota(shape, dim):
    return lax.broadcasted_iota(jnp.int32, shape, dim)


def hot(mask):
    return jnp.where(mask, 1.0, 0.0).astype(jnp.bfloat16)


def call(kernel, outs, args, flops, scalars=0):
    moved = sum(math.prod(x.shape) * x.dtype.itemsize for x in (*outs, *args))
    smem = [pl.BlockSpec(memory_space=pltpu.SMEM)] * scalars
    vmem = [pl.BlockSpec(memory_space=pltpu.VMEM)] * (len(args) - scalars)
    return pl.pallas_call(
        kernel,
        out_shape=outs,
        in_specs=smem + vmem,
        out_specs=[pl.BlockSpec(memory_space=pltpu.VMEM)] * len(outs),
        compiler_params=pltpu.CompilerParams(vmem_limit_bytes=40 * 2**20),
        cost_estimate=pl.CostEstimate(flops=flops, bytes_accessed=moved, transcendentals=0),
    )(*args)


def low(*shape):
    return jax.ShapeDtypeStruct(shape, jnp.bfloat16)


def pack_points_kernel(dev_ref, row_ref, x_ref, out_ref, slots_ref):
    n_dev, block, width = out_ref.shape
    cap = block - INFO_ROWS
    rows = x_ref.shape[0]
    dev = dev_ref[...]
    mine = iota((n_dev, rows), 0) == dev
    mine_f = jnp.where(mine, 1.0, 0.0)
    upto = hot(iota((rows, rows), 0) <= iota((rows, rows), 1))
    running = contract(mine_f.astype(jnp.bfloat16), upto, 1, 0)
    rank = (jnp.sum(running * mine_f, axis=0, keepdims=True) - 1.0).astype(jnp.int32)
    slots = dev * cap + rank
    slots_ref[...] = slots
    at_rank = hot(iota((LANES, rows), 0) % cap == rank)
    centred = (row_ref[...] - rows // 2).astype(jnp.float32)
    told = jnp.concatenate([mine_f * centred, mine_f], axis=0).astype(jnp.bfloat16)
    got = contract(told, at_rank, 1, 1)
    info = jnp.where(got[n_dev:] > 0.5, got[:n_dev], float(rows))
    per = 256 // cap
    for first in range(0, n_dev, per):
        pick = hot(iota((per * cap, rows), 0) + first * cap == slots)
        data = contract(pick, x_ref[...], 1, 0)
        for j in range(per):
            dest = first + j
            extra = jnp.broadcast_to(info[dest : dest + 1], (INFO_ROWS, LANES))
            extra = jnp.concatenate(
                [extra, jnp.zeros((INFO_ROWS, width - LANES), jnp.float32)], axis=1
            )
            out_ref[dest] = jnp.concatenate(
                [data[j * cap : (j + 1) * cap], extra], axis=0
            ).astype(jnp.bfloat16)


def pack_grads_kernel(slots_ref, x_ref, out_ref, back_ref):
    total = out_ref.shape[0]
    rows = x_ref.shape[0]
    pick = jnp.where(iota((total, rows), 0) == slots_ref[...], 1.0, 0.0)
    out_ref[...] = contract(pick.astype(jnp.bfloat16), x_ref[...], 1, 0).astype(jnp.bfloat16)
    back_ref[...] = pick.T.astype(jnp.bfloat16)


def place_points_kernel(got_ref, head_ref, tail_ref, table_ref, back_ref):
    n_dev, block, width = got_ref.shape
    cap = block - INFO_ROWS
    rows = table_ref.shape[0]
    half = rows // 2
    per = LANES // cap
    source = iota((1, LANES), 1) // cap
    centred = (iota((rows, LANES), 0) - half).astype(jnp.float32)
    parts, data = ([], [])
    for first in range(0, n_dev, per):
        at = jnp.zeros((1, LANES), jnp.float32)
        for j in range(per):
            info = got_ref[first + j][:, :LANES].astype(jnp.float32)[cap : cap + 1]
            at = jnp.where(source == j, info, at)
            if cap % 16 == 0:
                data.append(got_ref[first + j][:cap])
            else:
                data.append(got_ref[first + j].astype(jnp.float32)[:cap])
        parts.append(jnp.where(centred == at, 1.0, 0.0))
    table = jnp.concatenate(parts, axis=1)
    table_low = table.astype(jnp.bfloat16)
    placed = contract(
        table_low, jnp.concatenate(data, axis=0).astype(jnp.bfloat16), 1, 0
    ).astype(jnp.bfloat16)
    head_ref[...] = placed[:half]
    tail_ref[...] = placed[half:]
    table_ref[...] = table_low
    back_ref[...] = table.T.astype(jnp.bfloat16)


def place_grads_kernel(table_ref, got_ref, head_ref, tail_ref):
    half = head_ref.shape[0]
    placed = contract(table_ref[...], got_ref[...], 1, 0).astype(jnp.bfloat16)
    head_ref[...] = placed[:half]
    tail_ref[...] = placed[half:]


def pick_kernel(table_ref, head_ref, tail_ref, out_ref):
    own = jnp.concatenate([head_ref[...], tail_ref[...]], axis=0)
    out_ref[...] = contract(table_ref[...], own, 1, 0).astype(jnp.bfloat16)


def restore_kernel(table_ref, got_ref, out_ref):
    out_ref[...] = contract(table_ref[...], got_ref[...], 1, 0).astype(jnp.bfloat16)


def forward_kernel(
    tail_ref, next_ref, w_ref, w_kv_t_ref, qkv_ref, key_t_ref, attn_t_ref, probs_ref, points_t_ref
):
    width = w_ref.shape[0]
    head_dim = width // HEADS
    points = jnp.concatenate([tail_ref[...], next_ref[...]], axis=0)
    points_t_ref[...] = points.astype(jnp.float32).T.astype(jnp.bfloat16)
    qkv_ref[...] = contract(points, w_ref[...], 1, 0).astype(jnp.bfloat16)
    kv_t = contract(w_kv_t_ref[...], points, 1, 1).astype(jnp.bfloat16)
    key_t_ref[...] = kv_t[:width]
    side = iota((1, LANES), 1) // head_dim
    factor = math.log2(math.e) / math.sqrt(head_dim)
    for head in range(HEADS):
        first = head * head_dim // LANES * LANES
        within = head * head_dim % LANES // head_dim
        query = qkv_ref[:, first : first + LANES]
        query = jnp.where(side == within, query, jnp.zeros_like(query))
        key = qkv_ref[:, width + first : width + first + LANES]
        scores = contract(key, query, 1, 1)
        top = jnp.max(scores, axis=0, keepdims=True)
        weight = jnp.exp2((scores - top) * factor)
        probs = weight * (1.0 / jnp.sum(weight, axis=0, keepdims=True))
        probs_low = probs.astype(jnp.bfloat16)
        probs_ref[head] = probs_low
        value_t = kv_t[width + head * head_dim : width + (head + 1) * head_dim]
        attn_t_ref[head * head_dim : (head + 1) * head_dim, :] = contract(
            value_t, probs_low, 1, 0
        ).astype(jnp.bfloat16)


def backward_kernel(
    tail_ref, next_ref, w_out_ref, qkv_ref, key_t_ref, attn_t_ref, probs_ref, out_ref, query_t_ref
):
    width = w_out_ref.shape[0]
    head_dim = width // HEADS
    scale = 1.0 / math.sqrt(head_dim)
    grads = jnp.concatenate([tail_ref[...], next_ref[...]], axis=0)
    grad_attn = contract(grads, w_out_ref[...], 1, 1).astype(jnp.bfloat16)
    grad_attn_t = contract(w_out_ref[...], grads, 1, 1).astype(jnp.bfloat16)
    side = iota((1, LANES), 1) // head_dim
    for first in range(0, width, LANES):
        cols = slice(first, first + LANES)
        grad = grad_attn[:, cols]
        query = qkv_ref[:, cols]
        value = qkv_ref[:, 2 * width + first : 2 * width + first + LANES]
        grad_key = jnp.zeros((grad.shape[0], LANES), jnp.float32)
        grad_value = grad_key
        for within in range(LANES // head_dim):
            chans = slice(first + within * head_dim, first + (within + 1) * head_dim)
            probs = probs_ref[first // head_dim + within]
            delta = jnp.sum(
                grad_attn_t[chans].astype(jnp.float32) * attn_t_ref[chans, :].astype(jnp.float32),
                axis=0,
                keepdims=True,
            )
            grad_probs = contract(
                value, jnp.where(side == within, grad, jnp.zeros_like(grad)), 1, 1
            )
            grad_scores = (probs.astype(jnp.float32) * (grad_probs - delta)).astype(jnp.bfloat16)
            grad_value = jnp.where(side == within, contract(probs, grad, 1, 0), grad_value)
            grad_key = jnp.where(side == within, contract(grad_scores, query, 1, 0), grad_key)
            query_t_ref[chans, :] = contract(key_t_ref[chans, :], grad_scores, 1, 0) * scale
        out_ref[:, width + first : width + first + LANES] = (grad_key * scale).astype(jnp.bfloat16)
        out_ref[:, 2 * width + first : 2 * width + first + LANES] = grad_value.astype(jnp.bfloat16)
    out_ref[:, :width] = query_t_ref[...].T.astype(jnp.bfloat16)


def weights_kernel(side_ref, points_t_ref, attn_t_ref, grad_qkv_ref, tail_ref, next_ref, out_ref):
    rows = out_ref.shape[0]
    n_qkv = grad_qkv_ref.shape[1]
    from_row = pl.multiple_of(side_ref[0] * rows, rows)
    grads = jnp.concatenate([tail_ref[...], next_ref[...]], axis=0)
    out_ref[:, :n_qkv] = contract(
        points_t_ref[pl.ds(from_row, rows), :], grad_qkv_ref[...], 1, 0
    ).astype(out_ref.dtype)
    out_ref[:, n_qkv:] = contract(attn_t_ref[pl.ds(from_row, rows), :], grads, 1, 0).astype(
        out_ref.dtype
    )


def inputs_kernel(grad_qkv_ref, w_ref, next_ref, tail_ref):
    half = tail_ref.shape[0]
    tail_ref[...] = contract(grad_qkv_ref[:half, :], w_ref[...], 1, 1).astype(jnp.bfloat16)
    next_ref[...] = contract(grad_qkv_ref[half:, :], w_ref[...], 1, 1).astype(jnp.bfloat16)


def exchange(blocks):
    return lax.all_to_all(blocks, "curve", split_axis=0, concat_axis=0, tiled=True)


def swap(block, axis, mask):
    size = lax.axis_size(axis)
    return lax.ppermute(block, axis, [(i, i ^ mask) for i in range(size)])


def split_rows(rows, side):
    half = rows.shape[0] // 2
    keep = lax.dynamic_slice_in_dim(rows, side * half, half, 0)
    send = lax.dynamic_slice_in_dim(rows, (1 - side) * half, half, 0)
    return (keep, send.astype(jnp.bfloat16))


def join_rows(own, got, side):
    return jnp.concatenate([jnp.where(side == 0, own, got), jnp.where(side == 0, got, own)], axis=0)


def order_blocks(blocks, place):
    count = blocks.shape[0]
    tail = blocks.shape[1:]
    bit = 1
    while bit < count:
        pairs = blocks.reshape(count // (2 * bit), 2, bit, *tail)
        blocks = jnp.where((place & bit) != 0, pairs[:, ::-1], pairs).reshape(count, *tail)
        bit *= 2
    return blocks


def sum_devices(keep, send):
    me = lax.axis_index("curve")
    n_line = lax.axis_size("curve") // 4
    core, side_x, line, side_y = (me & 1, (me >> 1) & 1, me >> 2, lax.axis_index("dp"))
    part = keep + swap(send, "curve", 1).astype(jnp.float32)
    half = part.shape[0] // 2
    keep_a, send_a = split_rows(part[:half], side_x)
    keep_b, send_b = split_rows(part[half:], side_y)
    part_a = keep_a + swap(send_a, "curve", 2).astype(jnp.float32)
    part_b = keep_b + swap(send_b, "dp", 1).astype(jnp.float32)
    keep_a, send_a = split_rows(part_a, side_y)
    keep_b, send_b = split_rows(part_b, side_x)
    part_a = keep_a + swap(send_a, "dp", 1).astype(jnp.float32)
    part_b = keep_b + swap(send_b, "curve", 2).astype(jnp.float32)
    width = keep.shape[1]
    rows = part_a.shape[0] // n_line
    both = jnp.stack([part_a.reshape(n_line, rows, width), part_b.reshape(n_line, rows, width)], axis=1)
    mine = lax.dynamic_index_in_dim(both, line, 0, keepdims=False)
    others = [
        swap(
            lax.dynamic_index_in_dim(both, line ^ k, 0, keepdims=False).astype(jnp.bfloat16),
            "curve",
            4 * k,
        )
        for k in range(1, n_line)
    ]
    for other in others:
        mine = mine + other.astype(jnp.float32)
    mine = mine.astype(jnp.bfloat16)
    blocks = jnp.stack([mine] + [swap(mine, "curve", 4 * k) for k in range(1, n_line)])
    blocks = order_blocks(blocks, line)
    full_a = blocks[:, 0].reshape(n_line * rows, width)
    full_b = blocks[:, 1].reshape(n_line * rows, width)
    got_a = swap(full_a, "dp", 1)
    got_b = swap(full_b, "curve", 2)
    full_a = join_rows(full_a, got_a, side_y)
    full_b = join_rows(full_b, got_b, side_x)
    got_a = swap(full_a, "curve", 2)
    got_b = swap(full_b, "dp", 1)
    half_rows = jnp.concatenate([join_rows(full_a, got_a, side_x), join_rows(full_b, got_b, side_y)])
    return join_rows(half_rows, swap(half_rows, "curve", 1), core).astype(jnp.float32)


def on_device(points, grad_out, dest_dev, dest_row, w_qkv, w_out):
    rows, width = points.shape[1:]
    half = rows - PATCH // 2
    n_dev = lax.axis_size("curve")
    cap = 2 * rows // n_dev
    total = n_dev * cap
    place_flops = 2 * total * rows * width
    send_points, slots = call(
        pack_points_kernel,
        [low(n_dev, cap + INFO_ROWS, width), jax.ShapeDtypeStruct((1, rows), jnp.int32)],
        [dest_dev, dest_row, points[0]],
        place_flops,
    )
    got_points = exchange(send_points)
    send_grads, restore_table = call(
        pack_grads_kernel, [low(total, width), low(rows, total)], [slots, grad_out[0]], place_flops
    )
    got_grads = exchange(send_grads.reshape(n_dev, cap, width)).reshape(total, width)
    head, tail_points, place_table, pick_table = call(
        place_points_kernel,
        [low(rows - half, width), low(half, width), low(rows, total), low(total, rows)],
        [got_points],
        place_flops,
    )
    next_points = from_behind(head, "curve", -1)
    qkv, key_t, attn_t, probs, points_t = call(
        forward_kernel,
        [
            low(rows, 3 * width),
            low(width, rows),
            low(width, rows),
            low(HEADS, PATCH, PATCH),
            low(width, rows),
        ],
        [tail_points, next_points, w_qkv, w_qkv[:, width:].T],
        2 * rows * width * 5 * width + 16 * rows * rows * width,
    )
    head, tail_grads = call(
        place_grads_kernel,
        [low(rows - half, width), low(half, width)],
        [place_table, got_grads],
        place_flops,
    )
    next_grads = from_behind(head, "curve", -1)
    grad_qkv = pl.pallas_call(
        backward_kernel,
        out_shape=low(rows, 3 * width),
        in_specs=[pl.BlockSpec(memory_space=pltpu.VMEM)] * 7,
        out_specs=pl.BlockSpec(memory_space=pltpu.VMEM),
        scratch_shapes=[pltpu.VMEM((width, rows), jnp.float32)],
        compiler_params=pltpu.CompilerParams(vmem_limit_bytes=40 * 2**20),
        cost_estimate=pl.CostEstimate(
            flops=32 * rows * rows * width, bytes_accessed=8 * 2**20, transcendentals=0
        ),
    )(tail_grads, next_grads, w_out, qkv, key_t, attn_t, probs)
    core = (lax.axis_index("curve") & 1).reshape(1)
    sums = functools.partial(
        call,
        weights_kernel,
        flops=4 * rows * width * width,
        scalars=1,
    )
    operands = [points_t, attn_t, grad_qkv, tail_grads, next_grads]
    (send,) = sums([low(width // 2, 4 * width)], [1 - core, *operands])
    next_input, tail_input = call(
        inputs_kernel,
        [low(rows - half, width), low(half, width)],
        [grad_qkv, w_qkv],
        6 * rows * width * width,
    )
    head_input = from_behind(next_input, "curve", 1)
    (keep,) = sums(
        [jax.ShapeDtypeStruct((width // 2, 4 * width), jnp.float32)], [core, *operands]
    )
    (picked,) = call(
        pick_kernel, [low(total, width)], [pick_table, head_input, tail_input], place_flops
    )
    returned = exchange(picked.reshape(n_dev, cap, width)).reshape(total, width)
    (result,) = call(restore_kernel, [low(rows, width)], [restore_table, returned], place_flops)
    weights = sum_devices(keep, send)
    return (result[None], weights[:, : 3 * width], weights[:, 3 * width :])


def solution(mesh):
    placed = (
        P("dp", "curve", None),
        P("dp", "curve", None),
        P("dp", "curve"),
        P("dp", "curve"),
        P(),
        P(),
    )
    return jax.shard_map(
        on_device,
        mesh=mesh,
        in_specs=placed,
        out_specs=(P("dp", "curve", None), P(), P()),
        check_vma=False,
    )
```

```python
import functools
import math

import jax
import jax.numpy as jnp
from jax import lax
from jax.experimental import pallas as pl
from jax.experimental.pallas import tpu as pltpu
from jax.sharding import PartitionSpec as P

HEADS = 8
PATCH = 512
INFO_ROWS = 8
LANES = 128


def from_behind(block, axis, distance):
    devices = range(lax.axis_size(axis))
    route = [((i - distance) % len(devices), i) for i in devices]
    return lax.ppermute(block, axis, route)


def contract(left, right, left_dim, right_dim):
    return lax.dot_general(
        left, right, (((left_dim,), (right_dim,)), ((), ())), preferred_element_type=jnp.float32
    )


def iota(shape, dim):
    return lax.broadcasted_iota(jnp.int32, shape, dim)


def hot(mask):
    return jnp.where(mask, 1.0, 0.0).astype(jnp.bfloat16)


def call(kernel, outs, args, flops, scalars=0, scratch=(), mib=16):
    moved = sum(math.prod(x.shape) * x.dtype.itemsize for x in (*outs, *args))
    smem = [pl.BlockSpec(memory_space=pltpu.SMEM)] * scalars
    vmem = [pl.BlockSpec(memory_space=pltpu.VMEM)] * (len(args) - scalars)
    return pl.pallas_call(
        kernel,
        out_shape=outs,
        in_specs=smem + vmem,
        out_specs=[pl.BlockSpec(memory_space=pltpu.VMEM)] * len(outs),
        scratch_shapes=list(scratch),
        compiler_params=pltpu.CompilerParams(vmem_limit_bytes=mib * 2**20),
        cost_estimate=pl.CostEstimate(flops=flops, bytes_accessed=moved, transcendentals=0),
    )(*args)


def low(*shape):
    return jax.ShapeDtypeStruct(shape, jnp.bfloat16)


def wide(*shape):
    return jax.ShapeDtypeStruct(shape, jnp.float32)


def pack_points_kernel(dev_ref, row_ref, x_ref, out_ref, slots_ref):
    n_dev, block, width = out_ref.shape
    cap = block - INFO_ROWS
    rows = x_ref.shape[0]
    dev = dev_ref[...]
    mine = iota((n_dev, rows), 0) == dev
    mine_f = jnp.where(mine, 1.0, 0.0)
    upto = hot(iota((rows, rows), 0) <= iota((rows, rows), 1))
    running = contract(mine_f.astype(jnp.bfloat16), upto, 1, 0)
    rank = (jnp.sum(running * mine_f, axis=0, keepdims=True) - 1.0).astype(jnp.int32)
    slots = dev * cap + rank
    slots_ref[...] = slots
    at_rank = hot(iota((LANES, rows), 0) % cap == rank)
    centred = (row_ref[...] - rows // 2).astype(jnp.float32)
    told = jnp.concatenate([mine_f * centred, mine_f], axis=0).astype(jnp.bfloat16)
    got = contract(told, at_rank, 1, 1)
    info = jnp.where(got[n_dev:] > 0.5, got[:n_dev], float(rows))
    per = 256 // cap
    for first in range(0, n_dev, per):
        pick = hot(iota((per * cap, rows), 0) + first * cap == slots)
        data = contract(pick, x_ref[...], 1, 0)
        for j in range(per):
            dest = first + j
            extra = jnp.broadcast_to(info[dest : dest + 1], (INFO_ROWS, LANES))
            extra = jnp.concatenate(
                [extra, jnp.zeros((INFO_ROWS, width - LANES), jnp.float32)], axis=1
            )
            out_ref[dest] = jnp.concatenate(
                [data[j * cap : (j + 1) * cap], extra], axis=0
            ).astype(jnp.bfloat16)


def pack_grads_kernel(slots_ref, x_ref, out_ref, back_ref):
    total = out_ref.shape[0]
    rows = x_ref.shape[0]
    pick = jnp.where(iota((total, rows), 0) == slots_ref[...], 1.0, 0.0)
    out_ref[...] = contract(pick.astype(jnp.bfloat16), x_ref[...], 1, 0).astype(jnp.bfloat16)
    back_ref[...] = pick.T.astype(jnp.bfloat16)


def place_points_kernel(got_ref, head_ref, tail_ref, table_ref, back_ref):
    n_dev, block, width = got_ref.shape
    cap = block - INFO_ROWS
    rows = table_ref.shape[0]
    half = rows // 2
    per = LANES // cap
    source = iota((1, LANES), 1) // cap
    centred = (iota((rows, LANES), 0) - half).astype(jnp.float32)
    parts, data = ([], [])
    for first in range(0, n_dev, per):
        at = jnp.zeros((1, LANES), jnp.float32)
        for j in range(per):
            info = got_ref[first + j][:, :LANES].astype(jnp.float32)[cap : cap + 1]
            at = jnp.where(source == j, info, at)
            if cap % 16 == 0:
                data.append(got_ref[first + j][:cap])
            else:
                data.append(got_ref[first + j].astype(jnp.float32)[:cap])
        parts.append(jnp.where(centred == at, 1.0, 0.0))
    table = jnp.concatenate(parts, axis=1)
    table_low = table.astype(jnp.bfloat16)
    placed = contract(
        table_low, jnp.concatenate(data, axis=0).astype(jnp.bfloat16), 1, 0
    ).astype(jnp.bfloat16)
    head_ref[...] = placed[:half]
    tail_ref[...] = placed[half:]
    table_ref[...] = table_low
    back_ref[...] = table.T.astype(jnp.bfloat16)


def pick_kernel(table_ref, own_ref, from_before_ref, from_after_ref, out_ref):
    half = from_before_ref.shape[0]
    own = jnp.concatenate(
        [
            own_ref[:half, :] + from_before_ref[...].astype(jnp.float32),
            own_ref[half:, :] + from_after_ref[...].astype(jnp.float32),
        ],
        axis=0,
    ).astype(jnp.bfloat16)
    out_ref[...] = contract(table_ref[...], own, 1, 0).astype(jnp.bfloat16)


def restore_kernel(table_ref, got_ref, out_ref):
    out_ref[...] = contract(table_ref[...], got_ref[...], 1, 0).astype(jnp.bfloat16)


def forward_kernel(
    before_ref,
    head_ref,
    tail_ref,
    after_ref,
    w_ref,
    w_kv_t_ref,
    query_ref,
    kv_ref,
    key_t_ref,
    attn_t_ref,
    probs_ref,
    points_t_ref,
):
    width = w_ref.shape[0]
    head_dim = width // HEADS
    half = head_ref.shape[0]
    points = jnp.concatenate([before_ref[...], head_ref[...], tail_ref[...], after_ref[...]], axis=0)
    points_t_ref[...] = points.astype(jnp.float32).T.astype(jnp.bfloat16)
    query_ref[...] = contract(points[half : 3 * half], w_ref[:, :width], 1, 0).astype(jnp.bfloat16)
    kv_ref[...] = contract(points, w_ref[:, width:], 1, 0).astype(jnp.bfloat16)
    kv_t = contract(w_kv_t_ref[...], points, 1, 1).astype(jnp.bfloat16)
    key_t_ref[...] = kv_t[:width]
    side = iota((1, LANES), 1) // head_dim
    factor = math.log2(math.e) / math.sqrt(head_dim)
    for head in range(HEADS):
        first = head * head_dim // LANES * LANES
        within = head * head_dim % LANES // head_dim
        query = query_ref[:, first : first + LANES]
        query = jnp.where(side == within, query, jnp.zeros_like(query))
        key = kv_ref[:, first : first + LANES]
        scores = jnp.concatenate(
            [
                contract(key[: 2 * half], query[:half], 1, 1),
                contract(key[2 * half :], query[half:], 1, 1),
            ],
            axis=1,
        )
        top = jnp.max(scores, axis=0, keepdims=True)
        weight = jnp.exp2((scores - top) * factor)
        probs = weight * (1.0 / jnp.sum(weight, axis=0, keepdims=True))
        probs_low = probs.astype(jnp.bfloat16)
        probs_ref[head] = probs_low
        value_t = kv_t[width + head * head_dim : width + (head + 1) * head_dim]
        attn_t_ref[head * head_dim : (head + 1) * head_dim, :] = jnp.concatenate(
            [
                contract(value_t[:, : 2 * half], probs_low[:, :half], 1, 0),
                contract(value_t[:, 2 * half :], probs_low[:, half:], 1, 0),
            ],
            axis=1,
        ).astype(jnp.bfloat16)


def backward_kernel(
    table_ref,
    got_ref,
    w_out_ref,
    query_ref,
    kv_ref,
    key_t_ref,
    attn_t_ref,
    probs_ref,
    grads_ref,
    grad_query_ref,
    grad_kv_ref,
    query_t_ref,
):
    width = w_out_ref.shape[0]
    head_dim = width // HEADS
    half = query_ref.shape[0] // 2
    scale = 1.0 / math.sqrt(head_dim)
    grads = contract(table_ref[...], got_ref[...], 1, 0).astype(jnp.bfloat16)
    grads_ref[...] = grads
    grad_attn = contract(grads, w_out_ref[...], 1, 1).astype(jnp.bfloat16)
    grad_attn_t = contract(w_out_ref[...], grads, 1, 1).astype(jnp.bfloat16)
    side = iota((1, LANES), 1) // head_dim
    sides = ((slice(0, half), slice(0, 2 * half)), (slice(half, 2 * half), slice(2 * half, 4 * half)))
    for first in range(0, width, LANES):
        cols = slice(first, first + LANES)
        value_cols = slice(width + first, width + first + LANES)
        grad = grad_attn[:, cols]
        query = query_ref[:, cols]
        for mine, patch in sides:
            value = kv_ref[patch, value_cols]
            grad_key = jnp.zeros((2 * half, LANES), jnp.float32)
            grad_value = grad_key
            for within in range(LANES // head_dim):
                chans = slice(first + within * head_dim, first + (within + 1) * head_dim)
                probs = probs_ref[first // head_dim + within][:, mine]
                delta = jnp.sum(
                    grad_attn_t[chans, mine].astype(jnp.float32)
                    * attn_t_ref[chans, mine].astype(jnp.float32),
                    axis=0,
                    keepdims=True,
                )
                masked = jnp.where(side == within, grad[mine], jnp.zeros_like(grad[mine]))
                grad_probs = contract(value, masked, 1, 1)
                grad_scores = (probs.astype(jnp.float32) * (grad_probs - delta)).astype(jnp.bfloat16)
                grad_value = jnp.where(
                    side == within, contract(probs, grad[mine], 1, 0), grad_value
                )
                grad_key = jnp.where(
                    side == within, contract(grad_scores, query[mine], 1, 0), grad_key
                )
                query_t_ref[chans, mine] = (
                    contract(key_t_ref[chans, patch], grad_scores, 1, 0) * scale
                )
            grad_kv_ref[patch, cols] = (grad_key * scale).astype(jnp.bfloat16)
            grad_kv_ref[patch, value_cols] = grad_value.astype(jnp.bfloat16)
    grad_query_ref[...] = query_t_ref[...].T.astype(jnp.bfloat16)


def weights_kernel(
    side_ref, points_t_ref, attn_t_ref, grad_query_ref, grad_kv_ref, grads_ref, out_ref
):
    rows = out_ref.shape[0]
    own, width = grad_query_ref.shape
    half = own // 2
    from_row = pl.multiple_of(side_ref[0] * rows, rows)
    points_t = points_t_ref[pl.ds(from_row, rows), :]
    kind = out_ref.dtype
    out_ref[:, :width] = contract(
        points_t[:, half : 3 * half], grad_query_ref[...], 1, 0
    ).astype(kind)
    out_ref[:, width : 3 * width] = contract(points_t, grad_kv_ref[...], 1, 0).astype(kind)
    out_ref[:, 3 * width :] = contract(
        attn_t_ref[pl.ds(from_row, rows), :], grads_ref[...], 1, 0
    ).astype(kind)


def inputs_kernel(grad_query_ref, grad_kv_ref, w_ref, own_ref, before_ref, after_ref):
    half = before_ref.shape[0]
    width = w_ref.shape[0]
    w_kv = w_ref[:, width:]
    before_ref[...] = contract(grad_kv_ref[:half, :], w_kv, 1, 1).astype(jnp.bfloat16)
    after_ref[...] = contract(grad_kv_ref[3 * half :, :], w_kv, 1, 1).astype(jnp.bfloat16)
    own_ref[...] = contract(grad_query_ref[...], w_ref[:, :width], 1, 1) + contract(
        grad_kv_ref[half : 3 * half, :], w_kv, 1, 1
    )


def exchange(blocks):
    return lax.all_to_all(blocks, "curve", split_axis=0, concat_axis=0, tiled=True)


def swap(block, axis, mask):
    size = lax.axis_size(axis)
    return lax.ppermute(block, axis, [(i, i ^ mask) for i in range(size)])


def order_blocks(blocks, place):
    count = blocks.shape[0]
    tail = blocks.shape[1:]
    bit = 1
    while bit < count:
        pairs = blocks.reshape(count // (2 * bit), 2, bit, *tail)
        blocks = jnp.where((place & bit) != 0, pairs[:, ::-1], pairs).reshape(count, *tail)
        bit *= 2
    return blocks


def part_rows(total, side, keep_ref, send_ref):
    half = keep_ref.shape[0]
    keep_ref[...] = jnp.where(side == 0, total[:half], total[half:])
    send_ref[...] = jnp.where(side == 0, total[half:], total[:half]).astype(jnp.bfloat16)


def first_sum_kernel(sides_ref, kept_ref, got_ref, keep_a, send_a, keep_b, send_b):
    half = kept_ref.shape[0] // 2
    part_rows(
        kept_ref[:half, :] + got_ref[:half, :].astype(jnp.float32), sides_ref[0], keep_a, send_a
    )
    part_rows(
        kept_ref[half:, :] + got_ref[half:, :].astype(jnp.float32), sides_ref[1], keep_b, send_b
    )


def second_sum_kernel(
    sides_ref, kept_a_ref, got_a_ref, kept_b_ref, got_b_ref, keep_a, send_a, keep_b, send_b
):
    part_rows(
        kept_a_ref[...] + got_a_ref[...].astype(jnp.float32), sides_ref[1], keep_a, send_a
    )
    part_rows(
        kept_b_ref[...] + got_b_ref[...].astype(jnp.float32), sides_ref[0], keep_b, send_b
    )


def spread_kernel(place_ref, *refs):
    pieces, qkv_ref, out_ref = (refs[:-2], refs[-2], refs[-1])
    n_qkv = qkv_ref.shape[1]
    core, side_x, side_y, line, unit = (place_ref[i] for i in range(5))
    side = ((side_x, side_y), (side_y, side_x))
    piece_rows = pieces[0].shape[0]
    step = 8 if piece_rows % 16 == 0 else piece_rows
    for index, piece in enumerate(pieces):
        far_core, rest = divmod(index, 4)
        part, far_first = divmod(rest, 2)
        first, second = side[part]
        base = ((core ^ far_core) * 2 + part) * 2 + (first ^ far_first)
        values = piece[...].astype(jnp.float32)
        per = piece_rows // 2 // step
        for block in range(2 * per):
            far_second, at = divmod(block, per)
            row = ((base * 2 + (second ^ far_second)) * per + (line ^ at)) * step
            row = pl.multiple_of(row, step)
            data = values[block * step : (block + 1) * step]
            qkv_ref[pl.ds(row, step), :] = data[:, :n_qkv]
            out_ref[pl.ds(row, step), :] = data[:, n_qkv:]


def sum_devices(keep, send, sides, width_qkv):
    me = lax.axis_index("curve")
    n_line = lax.axis_size("curve") // 4
    line = me >> 2
    rows, width = keep.shape
    kept_a, send_a, kept_b, send_b = call(
        first_sum_kernel,
        [wide(rows // 4, width), low(rows // 4, width)] * 2,
        [sides, keep, swap(send, "curve", 1)],
        rows * width,
        scalars=1,
    )
    got_a = swap(send_a, "curve", 2)
    got_b = swap(send_b, "dp", 1)
    kept_a, send_a, kept_b, send_b = call(
        second_sum_kernel,
        [wide(rows // 8, width), low(rows // 8, width)] * 2,
        [sides, kept_a, got_a, kept_b, got_b],
        rows * width // 2,
        scalars=1,
    )
    part_a = kept_a + swap(send_a, "dp", 1).astype(jnp.float32)
    part_b = kept_b + swap(send_b, "curve", 2).astype(jnp.float32)
    rows = part_a.shape[0] // n_line
    both = jnp.stack([part_a.reshape(n_line, rows, width), part_b.reshape(n_line, rows, width)], axis=1)
    mine = lax.dynamic_index_in_dim(both, line, 0, keepdims=False)
    others = [
        swap(
            lax.dynamic_index_in_dim(both, line ^ k, 0, keepdims=False).astype(jnp.bfloat16),
            "curve",
            4 * k,
        )
        for k in range(1, n_line)
    ]
    for other in others:
        mine = mine + other.astype(jnp.float32)
    mine = mine.astype(jnp.bfloat16)
    blocks = jnp.stack([mine] + [swap(mine, "curve", 4 * k) for k in range(1, n_line)])
    place = line
    if rows != 8:
        blocks, place = (order_blocks(blocks, line), jnp.zeros_like(line))
    part_a = blocks[:, 0].reshape(n_line * rows, width)
    part_b = blocks[:, 1].reshape(n_line * rows, width)
    part_a = jnp.concatenate([part_a, swap(part_a, "dp", 1)])
    part_b = jnp.concatenate([part_b, swap(part_b, "curve", 2)])
    pieces = [part_a, swap(part_a, "curve", 2), part_b, swap(part_b, "dp", 1)]
    pieces += [swap(piece, "curve", 1) for piece in pieces]
    where = jnp.stack([me & 1, sides[0], sides[1], place, place])
    return call(
        spread_kernel,
        [wide(8 * part_a.shape[0], width_qkv), wide(8 * part_a.shape[0], width - width_qkv)],
        [where, *pieces],
        0,
        scalars=1,
    )


def on_device(points, grad_out, dest_dev, dest_row, w_qkv, w_out):
    rows, width = points.shape[1:]
    half = rows - PATCH // 2
    n_dev = lax.axis_size("curve")
    cap = 2 * rows // n_dev
    total = n_dev * cap
    place_flops = 2 * total * rows * width
    me = lax.axis_index("curve")
    core = (me & 1).reshape(1)
    sides = jnp.stack([(me >> 1) & 1, lax.axis_index("dp")])
    send_points, slots = call(
        pack_points_kernel,
        [low(n_dev, cap + INFO_ROWS, width), jax.ShapeDtypeStruct((1, rows), jnp.int32)],
        [dest_dev, dest_row, points[0]],
        place_flops,
    )
    got_points = exchange(send_points)
    send_grads, restore_table = call(
        pack_grads_kernel, [low(total, width), low(rows, total)], [slots, grad_out[0]], place_flops
    )
    got_grads = exchange(send_grads.reshape(n_dev, cap, width)).reshape(total, width)
    head, tail, place_table, pick_table = call(
        place_points_kernel,
        [low(half, width), low(half, width), low(rows, total), low(total, rows)],
        [got_points],
        place_flops,
    )
    after = from_behind(head, "curve", -1)
    before = from_behind(tail, "curve", 1)
    query, kv, key_t, attn_t, probs, points_t = call(
        forward_kernel,
        [
            low(rows, width),
            low(2 * rows, 2 * width),
            low(width, 2 * rows),
            low(width, rows),
            low(HEADS, PATCH, PATCH),
            low(width, 2 * rows),
        ],
        [before, head, tail, after, w_qkv, w_qkv[:, width:].T],
        2 * rows * width * 9 * width + 16 * rows * rows * width,
        mib=32,
    )
    grads, grad_query, grad_kv = call(
        backward_kernel,
        [low(rows, width), low(rows, width), low(2 * rows, 2 * width)],
        [place_table, got_grads, w_out, query, kv, key_t, attn_t, probs],
        32 * rows * rows * width,
        scratch=[pltpu.VMEM((width, rows), jnp.float32)],
        mib=32,
    )
    sums = functools.partial(call, weights_kernel, flops=6 * rows * width * width, scalars=1)
    operands = [points_t, attn_t, grad_query, grad_kv, grads]
    (send,) = sums([low(width // 2, 4 * width)], [1 - core, *operands])
    own_input, to_before, to_after = call(
        inputs_kernel,
        [wide(rows, width), low(half, width), low(half, width)],
        [grad_query, grad_kv, w_qkv],
        10 * rows * width * width,
    )
    (keep,) = sums([wide(width // 2, 4 * width)], [core, *operands])
    from_before = from_behind(to_after, "curve", 1)
    from_after = from_behind(to_before, "curve", -1)
    (picked,) = call(
        pick_kernel,
        [low(total, width)],
        [pick_table, own_input, from_before, from_after],
        place_flops,
    )
    returned = exchange(picked.reshape(n_dev, cap, width)).reshape(total, width)
    (result,) = call(restore_kernel, [low(rows, width)], [restore_table, returned], place_flops)
    weight_qkv, weight_out = sum_devices(keep, send, sides, 3 * width)
    return (result[None], weight_qkv, weight_out)


def solution(mesh):
    placed = (
        P("dp", "curve", None),
        P("dp", "curve", None),
        P("dp", "curve"),
        P("dp", "curve"),
        P(),
        P(),
    )
    return jax.shard_map(
        on_device,
        mesh=mesh,
        in_specs=placed,
        out_specs=(P("dp", "curve", None), P(), P()),
        check_vma=False,
    )
```

```python
import functools
import math

import jax
import jax.numpy as jnp
from jax import lax
from jax.experimental import pallas as pl
from jax.experimental.pallas import tpu as pltpu
from jax.sharding import PartitionSpec as P

HEADS = 8
PATCH = 512
INFO_ROWS = 8
GATE_FLOPS = 10**10
FORWARD_FLOPS = 10**11
SPREAD_FLOPS = 13 * 10**9
LANES = 128


def from_behind(block, axis, distance):
    devices = range(lax.axis_size(axis))
    route = [((i - distance) % len(devices), i) for i in devices]
    return lax.ppermute(block, axis, route)


def contract(left, right, left_dim, right_dim):
    return lax.dot_general(
        left, right, (((left_dim,), (right_dim,)), ((), ())), preferred_element_type=jnp.float32
    )


def iota(shape, dim):
    return lax.broadcasted_iota(jnp.int32, shape, dim)


def hot(mask):
    return jnp.where(mask, 1.0, 0.0).astype(jnp.bfloat16)


VMEM = pl.BlockSpec(memory_space=pltpu.VMEM)
SMEM = pl.BlockSpec(memory_space=pltpu.SMEM)
HBM = pl.BlockSpec(memory_space=pltpu.HBM)
ANY = pl.BlockSpec(memory_space=pl.ANY)


def low(*shape):
    return jax.ShapeDtypeStruct(shape, jnp.bfloat16)


def wide(*shape):
    return jax.ShapeDtypeStruct(shape, jnp.float32)


def space(shape):
    return pltpu.VMEM(shape.shape, shape.dtype)


def call(kernel, outs, args, flops, ins=None, out_specs=None, scratch=(), mib=16):
    moved = sum(math.prod(x.shape) * x.dtype.itemsize for x in (*outs, *args))
    return pl.pallas_call(
        kernel,
        out_shape=outs,
        in_specs=ins or [VMEM] * len(args),
        out_specs=out_specs or [VMEM] * len(outs),
        scratch_shapes=list(scratch),
        compiler_params=pltpu.CompilerParams(vmem_limit_bytes=mib * 2**20),
        cost_estimate=pl.CostEstimate(flops=flops, bytes_accessed=moved, transcendentals=0),
    )(*args)


def fetch(sources, places, sems, first=0):
    copies = [
        pltpu.make_async_copy(source, place, sems.at[first + i])
        for i, (source, place) in enumerate(zip(sources, places, strict=True))
    ]
    for copy in copies:
        copy.start()
    return copies


def gate(block, *others, flops=0):
    return pl.pallas_call(
        lambda *refs: None,
        out_shape=jax.ShapeDtypeStruct(block.shape, block.dtype),
        in_specs=[HBM] + [ANY] * len(others),
        out_specs=HBM,
        input_output_aliases={0: 0},
        cost_estimate=pl.CostEstimate(flops=flops, bytes_accessed=0, transcendentals=0),
    )(block, *others)


def pack_points_kernel(dev_hbm, row_hbm, x_hbm, out_ref, slots_ref, dev_ref, row_ref, x_ref, sems):
    copies = fetch([dev_hbm, row_hbm, x_hbm], [dev_ref, row_ref, x_ref], sems)
    n_dev, block, width = out_ref.shape
    cap = block - INFO_ROWS
    rows = x_ref.shape[0]
    copies[0].wait()
    dev = dev_ref[...]
    mine = iota((n_dev, rows), 0) == dev
    mine_f = jnp.where(mine, 1.0, 0.0)
    upto = hot(iota((rows, rows), 0) <= iota((rows, rows), 1))
    running = contract(mine_f.astype(jnp.bfloat16), upto, 1, 0)
    rank = (jnp.sum(running * mine_f, axis=0, keepdims=True) - 1.0).astype(jnp.int32)
    slots = dev * cap + rank
    slots_ref[...] = slots
    at_rank = hot(iota((LANES, rows), 0) % cap == rank)
    copies[1].wait()
    centred = (row_ref[...] - rows // 2).astype(jnp.float32)
    told = jnp.concatenate([mine_f * centred, mine_f], axis=0).astype(jnp.bfloat16)
    got = contract(told, at_rank, 1, 1)
    info = jnp.where(got[n_dev:] > 0.5, got[:n_dev], float(rows))
    per = 256 // cap
    copies[2].wait()
    for first in range(0, n_dev, per):
        pick = hot(iota((per * cap, rows), 0) + first * cap == slots)
        data = contract(pick, x_ref[...], 1, 0)
        for j in range(per):
            dest = first + j
            extra = jnp.broadcast_to(info[dest : dest + 1], (INFO_ROWS, LANES))
            extra = jnp.concatenate(
                [extra, jnp.zeros((INFO_ROWS, width - LANES), jnp.float32)], axis=1
            )
            out_ref[dest] = jnp.concatenate(
                [data[j * cap : (j + 1) * cap], extra], axis=0
            ).astype(jnp.bfloat16)


def pack_grads_kernel(slots_ref, x_ref, out_ref, back_ref):
    total = out_ref.shape[0]
    rows = x_ref.shape[0]
    pick = jnp.where(iota((total, rows), 0) == slots_ref[...], 1.0, 0.0)
    out_ref[...] = contract(pick.astype(jnp.bfloat16), x_ref[...], 1, 0).astype(jnp.bfloat16)
    back_ref[...] = pick.T.astype(jnp.bfloat16)


def place_points_kernel(got_ref, head_ref, tail_ref, at_ref):
    n_dev, block, width = got_ref.shape
    cap = block - INFO_ROWS
    half = head_ref.shape[0]
    rows = 2 * half
    per = LANES // cap
    source = iota((1, LANES), 1) // cap
    centred = (iota((rows, LANES), 0) - half).astype(jnp.float32)
    parts, data = ([], [])
    for first in range(0, n_dev, per):
        at = jnp.zeros((1, LANES), jnp.float32)
        for j in range(per):
            info = got_ref[first + j][:, :LANES].astype(jnp.float32)[cap : cap + 1]
            at = jnp.where(source == j, info, at)
            if cap % 16 == 0:
                data.append(got_ref[first + j][:cap])
            else:
                data.append(got_ref[first + j].astype(jnp.float32)[:cap])
        at_ref[first // per : first // per + 1, :] = at
        parts.append(hot(centred == at))
    placed = contract(
        jnp.concatenate(parts, axis=1), jnp.concatenate(data, axis=0).astype(jnp.bfloat16), 1, 0
    ).astype(jnp.bfloat16)
    head_ref[...] = placed[:half]
    tail_ref[...] = placed[half:]


def place_table(at_ref, rows):
    centred = (iota((rows, LANES), 0) - rows // 2).astype(jnp.float32)
    parts = [
        jnp.where(centred == at_ref[g : g + 1, :], 1.0, 0.0) for g in range(at_ref.shape[0])
    ]
    return jnp.concatenate(parts, axis=1)


def pick_kernel(table_ref, own_hbm, from_before_ref, from_after_ref, out_ref, own_ref, sems):
    (copy,) = fetch([own_hbm], [own_ref], sems)
    copy.wait()
    half = from_before_ref.shape[0]
    own = jnp.concatenate(
        [
            own_ref[:half, :] + from_before_ref[...].astype(jnp.float32),
            own_ref[half:, :] + from_after_ref[...].astype(jnp.float32),
        ],
        axis=0,
    ).astype(jnp.bfloat16)
    out_ref[...] = contract(table_ref[...], own, 1, 0).astype(jnp.bfloat16)


def restore_kernel(table_ref, got_ref, out_ref):
    out_ref[...] = contract(table_ref[...], got_ref[...], 1, 0).astype(jnp.bfloat16)


def forward_kernel(
    at_ref,
    before_hbm,
    head_hbm,
    tail_hbm,
    after_hbm,
    w_hbm,
    w_kv_t_hbm,
    query_hbm,
    kv_hbm,
    key_t_hbm,
    attn_t_hbm,
    probs_hbm,
    points_t_hbm,
    table_hbm,
    points_ref,
    w_ref,
    w_kv_t_ref,
    query_ref,
    kv_ref,
    key_t_ref,
    attn_t_ref,
    probs_ref,
    points_t_ref,
    table_ref,
    sems,
):
    width = w_ref.shape[0]
    head_dim = width // HEADS
    half = points_ref.shape[0] // 4
    quarters = [points_ref.at[pl.ds(i * half, half), :] for i in range(4)]
    copies = fetch(
        [before_hbm, head_hbm, tail_hbm, after_hbm, w_hbm, w_kv_t_hbm],
        [*quarters, w_ref, w_kv_t_ref],
        sems,
    )
    table_ref[...] = place_table(at_ref, 2 * half).T.astype(jnp.bfloat16)
    stores = fetch([table_ref], [table_hbm], sems, 6)
    for copy in copies:
        copy.wait()
    points = points_ref[...]
    query_ref[...] = contract(points[half : 3 * half], w_ref[:, :width], 1, 0).astype(jnp.bfloat16)
    kv_ref[...] = contract(points, w_ref[:, width:], 1, 0).astype(jnp.bfloat16)
    kv_t = contract(w_kv_t_ref[...], points, 1, 1).astype(jnp.bfloat16)
    key_t_ref[...] = kv_t[:width]
    points_t_ref[...] = points.astype(jnp.float32).T.astype(jnp.bfloat16)
    stores += fetch(
        [query_ref, kv_ref, key_t_ref, points_t_ref],
        [query_hbm, kv_hbm, key_t_hbm, points_t_hbm],
        sems,
        7,
    )
    side = iota((1, LANES), 1) // head_dim
    factor = math.log2(math.e) / math.sqrt(head_dim)
    for head in range(HEADS):
        first = head * head_dim // LANES * LANES
        within = head * head_dim % LANES // head_dim
        query = query_ref[:, first : first + LANES]
        query = jnp.where(side == within, query, jnp.zeros_like(query))
        key = kv_ref[:, first : first + LANES]
        scores = jnp.concatenate(
            [
                contract(key[: 2 * half], query[:half], 1, 1),
                contract(key[2 * half :], query[half:], 1, 1),
            ],
            axis=1,
        )
        top = jnp.max(scores, axis=0, keepdims=True)
        weight = jnp.exp2((scores - top) * factor)
        probs = weight * (1.0 / jnp.sum(weight, axis=0, keepdims=True))
        probs_low = probs.astype(jnp.bfloat16)
        probs_ref[head] = probs_low
        stores += fetch([probs_ref.at[head]], [probs_hbm.at[head]], sems, 12 + head)
        value_t = kv_t[width + head * head_dim : width + (head + 1) * head_dim]
        attn_t_ref[head * head_dim : (head + 1) * head_dim, :] = jnp.concatenate(
            [
                contract(value_t[:, : 2 * half], probs_low[:, :half], 1, 0),
                contract(value_t[:, 2 * half :], probs_low[:, half:], 1, 0),
            ],
            axis=1,
        ).astype(jnp.bfloat16)
    stores += fetch([attn_t_ref], [attn_t_hbm], sems, 11)
    for store in stores:
        store.wait()


def weights(points_t, attn_t, grad_query, grad_kv, grads):
    half = grads.shape[0] // 2
    return (
        contract(points_t[:, half : 3 * half], grad_query, 1, 0),
        contract(points_t, grad_kv, 1, 0),
        contract(attn_t, grads, 1, 0),
    )


def backward_kernel(
    core_ref,
    at_ref,
    got_hbm,
    w_out_hbm,
    query_hbm,
    kv_hbm,
    key_t_hbm,
    attn_t_hbm,
    points_t_hbm,
    w_hbm,
    probs_hbm,
    send_ref,
    keep_ref,
    own_hbm,
    before_ref,
    after_ref,
    got_ref,
    w_out_ref,
    query_ref,
    kv_ref,
    key_t_ref,
    attn_t_ref,
    points_t_ref,
    w_ref,
    probs_ref,
    grad_query_ref,
    grad_kv_ref,
    query_t_ref,
    own_ref,
    sems,
):
    width = w_out_ref.shape[0]
    head_dim = width // HEADS
    half = query_ref.shape[0] // 2
    scale = 1.0 / math.sqrt(head_dim)
    copies = fetch(
        [got_hbm, w_out_hbm, attn_t_hbm, kv_hbm, query_hbm, key_t_hbm],
        [got_ref, w_out_ref, attn_t_ref, kv_ref, query_ref, key_t_ref],
        sems,
    )
    probs_copies = []
    for head in range(HEADS):
        probs_copies += fetch([probs_hbm.at[head]], [probs_ref.at[head]], sems, 8 + head)
    late = fetch([points_t_hbm, w_hbm], [points_t_ref, w_ref], sems, 6)
    table = place_table(at_ref, 2 * half).astype(jnp.bfloat16)
    copies[0].wait()
    grads = contract(table, got_ref[...], 1, 0).astype(jnp.bfloat16)
    copies[1].wait()
    grad_attn = contract(grads, w_out_ref[...], 1, 1).astype(jnp.bfloat16)
    grad_attn_t = contract(w_out_ref[...], grads, 1, 1).astype(jnp.bfloat16)
    for copy in copies[2:]:
        copy.wait()
    side = iota((1, LANES), 1) // head_dim
    sides = ((slice(0, half), slice(0, 2 * half)), (slice(half, 2 * half), slice(2 * half, 4 * half)))
    for first in range(0, width, LANES):
        cols = slice(first, first + LANES)
        value_cols = slice(width + first, width + first + LANES)
        grad = grad_attn[:, cols]
        query = query_ref[:, cols]
        for head in range(first // head_dim, (first + LANES) // head_dim):
            probs_copies[head].wait()
        for mine, patch in sides:
            value = kv_ref[patch, value_cols]
            grad_key = jnp.zeros((2 * half, LANES), jnp.float32)
            grad_value = grad_key
            for within in range(LANES // head_dim):
                chans = slice(first + within * head_dim, first + (within + 1) * head_dim)
                probs = probs_ref[first // head_dim + within][:, mine]
                delta = jnp.sum(
                    grad_attn_t[chans, mine].astype(jnp.float32)
                    * attn_t_ref[chans, mine].astype(jnp.float32),
                    axis=0,
                    keepdims=True,
                )
                masked = jnp.where(side == within, grad[mine], jnp.zeros_like(grad[mine]))
                grad_probs = contract(value, masked, 1, 1)
                grad_scores = (probs.astype(jnp.float32) * (grad_probs - delta)).astype(jnp.bfloat16)
                grad_value = jnp.where(
                    side == within, contract(probs, grad[mine], 1, 0), grad_value
                )
                grad_key = jnp.where(
                    side == within, contract(grad_scores, query[mine], 1, 0), grad_key
                )
                query_t_ref[chans, mine] = (
                    contract(key_t_ref[chans, patch], grad_scores, 1, 0) * scale
                )
            grad_kv_ref[patch, cols] = (grad_key * scale).astype(jnp.bfloat16)
            grad_kv_ref[patch, value_cols] = grad_value.astype(jnp.bfloat16)
    grad_query_ref[...] = query_t_ref[...].T.astype(jnp.bfloat16)
    for copy in late:
        copy.wait()
    w_kv = w_ref[:, width:]
    own_ref[...] = contract(grad_query_ref[...], w_ref[:, :width], 1, 1) + contract(
        grad_kv_ref[half : 3 * half, :], w_kv, 1, 1
    )
    (store,) = fetch([own_ref], [own_hbm], sems, 8 + HEADS)
    before_ref[...] = contract(grad_kv_ref[:half, :], w_kv, 1, 1).astype(jnp.bfloat16)
    after_ref[...] = contract(grad_kv_ref[3 * half :, :], w_kv, 1, 1).astype(jnp.bfloat16)
    rows = width // 2
    for side, out_ref in ((core_ref[0], keep_ref), (1 - core_ref[0], send_ref)):
        from_row = pl.multiple_of(side * rows, rows)
        of_query, of_kv, of_out = weights(
            points_t_ref[pl.ds(from_row, rows), :],
            attn_t_ref[pl.ds(from_row, rows), :],
            grad_query_ref[...],
            grad_kv_ref[...],
            grads,
        )
        out_ref[:, :width] = of_query.astype(out_ref.dtype)
        out_ref[:, width : 3 * width] = of_kv.astype(out_ref.dtype)
        out_ref[:, 3 * width :] = of_out.astype(out_ref.dtype)
    store.wait()


def exchange(blocks):
    return lax.all_to_all(blocks, "curve", split_axis=0, concat_axis=0, tiled=True)


def swap(block, axis, mask):
    size = lax.axis_size(axis)
    return lax.ppermute(block, axis, [(i, i ^ mask) for i in range(size)])


def order_blocks(blocks, place):
    count = blocks.shape[0]
    tail = blocks.shape[1:]
    bit = 1
    while bit < count:
        pairs = blocks.reshape(count // (2 * bit), 2, bit, *tail)
        blocks = jnp.where((place & bit) != 0, pairs[:, ::-1], pairs).reshape(count, *tail)
        bit *= 2
    return blocks


def part_rows(total, side, keep_ref, send_ref):
    half = keep_ref.shape[0]
    keep_ref[...] = jnp.where(side == 0, total[:half], total[half:])
    send_ref[...] = jnp.where(side == 0, total[half:], total[:half]).astype(jnp.bfloat16)


def first_sum_kernel(sides_ref, kept_ref, got_ref, keep_a, send_a, keep_b, send_b):
    half = kept_ref.shape[0] // 2
    part_rows(
        kept_ref[:half, :] + got_ref[:half, :].astype(jnp.float32), sides_ref[0], keep_a, send_a
    )
    part_rows(
        kept_ref[half:, :] + got_ref[half:, :].astype(jnp.float32), sides_ref[1], keep_b, send_b
    )


def second_sum_kernel(
    sides_ref, kept_a_ref, got_a_ref, kept_b_ref, got_b_ref, keep_a, send_a, keep_b, send_b
):
    part_rows(
        kept_a_ref[...] + got_a_ref[...].astype(jnp.float32), sides_ref[1], keep_a, send_a
    )
    part_rows(
        kept_b_ref[...] + got_b_ref[...].astype(jnp.float32), sides_ref[0], keep_b, send_b
    )


def third_sum_kernel(
    line_ref, kept_a_ref, got_a_ref, kept_b_ref, got_b_ref, _, mine_ref, *refs
):
    sends, total_ref = (refs[:-1], refs[-1])
    rows = mine_ref.shape[0] // 2
    half = kept_a_ref.shape[0]
    total_ref[:half, :] = kept_a_ref[...] + got_a_ref[...].astype(jnp.float32)
    total_ref[half:, :] = kept_b_ref[...] + got_b_ref[...].astype(jnp.float32)
    for distance, out_ref in enumerate((mine_ref, *sends)):
        at = pl.multiple_of((line_ref[0] ^ distance) * rows, rows)
        out_ref[...] = jnp.concatenate(
            [total_ref[pl.ds(at, rows), :], total_ref[pl.ds(half + at, rows), :]], axis=0
        ).astype(out_ref.dtype)


def spread_kernel(n_line, place_ref, *refs):
    pieces, qkv_ref, out_ref = (refs[:-2], refs[-2], refs[-1])
    n_qkv = qkv_ref.shape[1]
    core, side_x, side_y, line = (place_ref[i] for i in range(4))
    rows = qkv_ref.shape[0] // (16 * n_line)
    for index, piece in enumerate(pieces):
        near_x, near_y = (side_x ^ (index & 1), side_y ^ (index >> 1 & 1))
        near_core = core ^ (index >> 2)
        values = piece[...].astype(jnp.float32)
        for block in range(2 * n_line):
            distance, part = divmod(block, 2)
            first, second = ((near_x, near_y), (near_y, near_x))[part]
            unit = (((near_core * 2 + part) * 2 + first) * 2 + second) * n_line + (line ^ distance)
            row = pl.multiple_of(unit * rows, rows)
            data = values[block * rows : (block + 1) * rows]
            qkv_ref[pl.ds(row, rows), :] = data[:, :n_qkv]
            out_ref[pl.ds(row, rows), :] = data[:, n_qkv:]


def sum_start(keep, send, sides, ready):
    n_line = lax.axis_size("curve") // 4
    line = lax.axis_index("curve") >> 2
    rows, width = keep.shape
    scalar = [SMEM] + [VMEM] * 4
    kept_a, send_a, kept_b, send_b = call(
        first_sum_kernel,
        [wide(rows // 4, width), low(rows // 4, width)] * 2,
        [sides, keep, swap(send, "curve", 1)],
        rows * width,
        scalar[:3],
    )
    got_a = swap(send_a, "curve", 2)
    got_b = swap(send_b, "dp", 1)
    kept_a, send_a, kept_b, send_b = call(
        second_sum_kernel,
        [wide(rows // 8, width), low(rows // 8, width)] * 2,
        [sides, kept_a, got_a, kept_b, got_b],
        rows * width // 2,
        scalar,
    )
    got_a = swap(send_a, "dp", 1)
    got_b = swap(send_b, "curve", 2)
    rows = kept_a.shape[0] // n_line
    if rows % 8 == 0:
        mine, *sends = call(
            third_sum_kernel,
            [wide(2 * rows, width)] + [low(2 * rows, width)] * (n_line - 1),
            [line.reshape(1), kept_a, got_a, kept_b, got_b, ready],
            kept_a.size,
            [*scalar, ANY],
            scratch=[pltpu.VMEM((2 * n_line * rows, width), jnp.float32)],
        )
    else:
        part_a = (kept_a + got_a.astype(jnp.float32)).reshape(n_line, rows, width)
        part_b = (kept_b + got_b.astype(jnp.float32)).reshape(n_line, rows, width)
        both = jnp.concatenate([part_a, part_b], axis=1)
        mine, *sends = [
            lax.dynamic_index_in_dim(both, line ^ k, 0, keepdims=False) for k in range(n_line)
        ]
        sends = [block.astype(jnp.bfloat16) for block in sends]
    for k, block in enumerate(sends):
        mine = mine + swap(block, "curve", 4 * (k + 1)).astype(jnp.float32)
    mine = mine.astype(jnp.bfloat16)
    blocks = [mine] + [swap(mine, "curve", 4 * k) for k in range(1, n_line)]
    if rows % 8 == 0:
        return (jnp.concatenate(blocks, axis=0), line)
    blocks = order_blocks(jnp.stack(blocks), line).reshape(2 * n_line * rows, width)
    return (blocks, jnp.zeros_like(line))


def sum_finish(own, line, sides, width_qkv):
    rows, width = own.shape
    over_x = swap(own, "curve", 2)
    over_y = swap(own, "dp", 1)
    pieces = [own, over_x, over_y, swap(over_x, "dp", 1)]
    pieces += [swap(piece, "curve", 1) for piece in pieces]
    where = jnp.stack([lax.axis_index("curve") & 1, sides[0], sides[1], line])
    return call(
        functools.partial(spread_kernel, lax.axis_size("curve") // 4),
        [wide(8 * rows, width_qkv), wide(8 * rows, width - width_qkv)],
        [where, *pieces],
        SPREAD_FLOPS,
        [SMEM] + [VMEM] * 8,
    )


def on_device(points, grad_out, dest_dev, dest_row, w_qkv, w_out):
    rows, width = points.shape[1:]
    half = rows - PATCH // 2
    n_dev = lax.axis_size("curve")
    cap = 2 * rows // n_dev
    total = n_dev * cap
    place_flops = 2 * total * rows * width
    me = lax.axis_index("curve")
    core = (me & 1).reshape(1)
    sides = jnp.stack([(me >> 1) & 1, lax.axis_index("dp")])
    ids = jax.ShapeDtypeStruct((1, rows), jnp.int32)
    send_points, slots = call(
        pack_points_kernel,
        [low(n_dev, cap + INFO_ROWS, width), ids],
        [dest_dev, dest_row, points[0]],
        place_flops,
        [HBM] * 3,
        scratch=[space(ids), space(ids), space(low(rows, width)), pltpu.SemaphoreType.DMA((3,))],
        mib=60,
    )
    got_points = exchange(send_points)
    send_grads, restore_table = call(
        pack_grads_kernel, [low(total, width), low(rows, total)], [slots, grad_out[0]], place_flops
    )
    head, tail, at = call(
        place_points_kernel,
        [low(half, width), low(half, width), wide(total // LANES, LANES)],
        [got_points],
        place_flops,
    )
    after = from_behind(head, "curve", -1)
    before = from_behind(tail, "curve", 1)
    send_grads = gate(send_grads, at, flops=GATE_FLOPS)
    got_grads = exchange(send_grads.reshape(n_dev, cap, width)).reshape(total, width)
    saved = [
        low(rows, width),
        low(2 * rows, 2 * width),
        low(width, 2 * rows),
        low(width, rows),
        low(HEADS, PATCH, PATCH),
        low(width, 2 * rows),
        low(total, rows),
    ]
    query, kv, key_t, attn_t, probs, points_t, pick_table = call(
        forward_kernel,
        saved,
        [at, before, head, tail, after, w_qkv, w_qkv[:, width:].T],
        FORWARD_FLOPS,
        [VMEM] + [HBM] * 6,
        [HBM] * len(saved),
        [space(low(2 * rows, width)), space(low(width, 3 * width)), space(low(2 * width, width))]
        + [space(x) for x in saved]
        + [pltpu.SemaphoreType.DMA((12 + HEADS,))],
        60,
    )
    held = [got_grads, w_out, query, kv, key_t, attn_t, points_t, w_qkv, probs]
    send, keep, own_input, to_before, to_after = call(
        backward_kernel,
        [
            low(width // 2, 4 * width),
            wide(width // 2, 4 * width),
            wide(rows, width),
            low(half, width),
            low(half, width),
        ],
        [core, at, *held],
        32 * rows * rows * width + 22 * rows * width * width,
        [SMEM, VMEM] + [HBM] * len(held),
        [VMEM, VMEM, HBM, VMEM, VMEM],
        [space(x) for x in held]
        + [
            space(low(rows, width)),
            space(low(2 * rows, 2 * width)),
            space(wide(width, rows)),
            space(wide(rows, width)),
            pltpu.SemaphoreType.DMA((9 + HEADS,)),
        ],
        60,
    )
    from_before = from_behind(to_after, "curve", 1)
    from_after = from_behind(to_before, "curve", -1)
    (picked,) = call(
        pick_kernel,
        [low(total, width)],
        [pick_table, own_input, from_before, from_after],
        place_flops,
        [VMEM, HBM, VMEM, VMEM],
        scratch=[space(wide(rows, width)), pltpu.SemaphoreType.DMA((1,))],
    )
    gathered, line = sum_start(keep, send, sides, picked)
    picked = gate(picked, gathered, flops=GATE_FLOPS)
    returned = exchange(picked.reshape(n_dev, cap, width)).reshape(total, width)
    weight_qkv, weight_out = sum_finish(gathered, line, sides, 3 * width)
    (result,) = call(restore_kernel, [low(rows, width)], [restore_table, returned], place_flops)
    return (result[None], weight_qkv, weight_out)


def solution(mesh):
    placed = (
        P("dp", "curve", None),
        P("dp", "curve", None),
        P("dp", "curve"),
        P("dp", "curve"),
        P(),
        P(),
    )
    return jax.shard_map(
        on_device,
        mesh=mesh,
        in_specs=placed,
        out_specs=(P("dp", "curve", None), P(), P()),
        check_vma=False,
    )
```

```python
import functools
import math

import jax
import jax.numpy as jnp
from jax import lax
from jax.experimental import pallas as pl
from jax.experimental.pallas import tpu as pltpu
from jax.sharding import PartitionSpec as P

HEADS = 8
PATCH = 512
INFO_ROWS = 8
GATE_FLOPS = 10**10
FORWARD_FLOPS = 10**11
SPREAD_FLOPS = 16 * 10**9
LANES = 128


def contract(left, right, left_dim, right_dim):
    return lax.dot_general(
        left, right, (((left_dim,), (right_dim,)), ((), ())), preferred_element_type=jnp.float32
    )


def iota(shape, dim):
    return lax.broadcasted_iota(jnp.int32, shape, dim)


def hot(mask):
    return jnp.where(mask, 1.0, 0.0).astype(jnp.bfloat16)


VMEM = pl.BlockSpec(memory_space=pltpu.VMEM)
SMEM = pl.BlockSpec(memory_space=pltpu.SMEM)
HBM = pl.BlockSpec(memory_space=pltpu.HBM)
ANY = pl.BlockSpec(memory_space=pl.ANY)


def low(*shape):
    return jax.ShapeDtypeStruct(shape, jnp.bfloat16)


def wide(*shape):
    return jax.ShapeDtypeStruct(shape, jnp.float32)


def space(shape):
    return pltpu.VMEM(shape.shape, shape.dtype)


def call(kernel, outs, args, flops, ins=None, out_specs=None, scratch=(), mib=16):
    moved = sum(math.prod(x.shape) * x.dtype.itemsize for x in (*outs, *args))
    return pl.pallas_call(
        kernel,
        out_shape=outs,
        in_specs=ins or [VMEM] * len(args),
        out_specs=out_specs or [VMEM] * len(outs),
        scratch_shapes=list(scratch),
        compiler_params=pltpu.CompilerParams(vmem_limit_bytes=mib * 2**20),
        cost_estimate=pl.CostEstimate(flops=flops, bytes_accessed=moved, transcendentals=0),
    )(*args)


def fetch(sources, places, sems, first=0):
    copies = [
        pltpu.make_async_copy(source, place, sems.at[first + i])
        for i, (source, place) in enumerate(zip(sources, places, strict=True))
    ]
    for copy in copies:
        copy.start()
    return copies


def gate(block, *others, flops=0):
    return pl.pallas_call(
        lambda *refs: None,
        out_shape=jax.ShapeDtypeStruct(block.shape, block.dtype),
        in_specs=[HBM] + [ANY] * len(others),
        out_specs=HBM,
        input_output_aliases={0: 0},
        cost_estimate=pl.CostEstimate(flops=flops, bytes_accessed=0, transcendentals=0),
    )(block, *others)


def pack_points_kernel(dev_hbm, row_hbm, x_hbm, out_ref, slots_ref, dev_ref, row_ref, x_ref, sems):
    copies = fetch([dev_hbm, row_hbm, x_hbm], [dev_ref, row_ref, x_ref], sems)
    n_dev, block, _ = out_ref.shape
    rows, width = x_ref.shape
    cap = (block - INFO_ROWS) * LANES // width
    copies[0].wait()
    dev = dev_ref[...]
    mine = iota((n_dev, rows), 0) == dev
    mine_f = jnp.where(mine, 1.0, 0.0)
    upto = hot(iota((rows, rows), 0) <= iota((rows, rows), 1))
    running = contract(mine_f.astype(jnp.bfloat16), upto, 1, 0)
    rank = (jnp.sum(running * mine_f, axis=0, keepdims=True) - 1.0).astype(jnp.int32)
    slots = dev * cap + rank
    slots_ref[...] = slots
    at_rank = hot(iota((LANES, rows), 0) % cap == rank)
    copies[1].wait()
    centred = (row_ref[...] - rows // 2).astype(jnp.float32)
    told = jnp.concatenate([mine_f * centred, mine_f], axis=0).astype(jnp.bfloat16)
    got = contract(told, at_rank, 1, 1)
    info = jnp.where(got[n_dev:] > 0.5, got[:n_dev], float(rows))
    per = 256 // cap
    copies[2].wait()
    for first in range(0, n_dev, per):
        pick = hot(iota((per * cap, rows), 0) + first * cap == slots)
        data = contract(pick, x_ref[...], 1, 0)
        for j in range(per):
            dest = first + j
            stack = [
                data[j * cap : (j + 1) * cap, col : col + LANES] for col in range(0, width, LANES)
            ]
            stack.append(jnp.broadcast_to(info[dest : dest + 1], (INFO_ROWS, LANES)))
            out_ref[dest] = jnp.concatenate(stack, axis=0).astype(jnp.bfloat16)


def pack_grads_kernel(slots_ref, x_ref, out_ref, back_ref):
    total = out_ref.shape[0]
    rows = x_ref.shape[0]
    pick = jnp.where(iota((total, rows), 0) == slots_ref[...], 1.0, 0.0)
    out_ref[...] = contract(pick.astype(jnp.bfloat16), x_ref[...], 1, 0).astype(jnp.bfloat16)
    back_ref[...] = pick.T.astype(jnp.bfloat16)


def place_points_kernel(core_ref, got_ref, own_ref, near_ref, far_ref, at_ref):
    n_dev, block, _ = got_ref.shape
    rows, width = own_ref.shape
    cap = (block - INFO_ROWS) * LANES // width
    half = rows // 2
    per = LANES // cap
    source = iota((1, LANES), 1) // cap
    centred = (iota((rows, LANES), 0) - half).astype(jnp.float32)
    parts, data = ([], [])
    for first in range(0, n_dev, per):
        at = jnp.zeros((1, LANES), jnp.float32)
        for j in range(per):
            got = got_ref[first + j]
            info = got.astype(jnp.float32)[block - INFO_ROWS : block - INFO_ROWS + 1]
            at = jnp.where(source == j, info, at)
            if cap % 16:
                got = got.astype(jnp.float32)
            cols = [got[i * cap : (i + 1) * cap] for i in range(width // LANES)]
            data.append(jnp.concatenate(cols, axis=1))
        at_ref[first // per : first // per + 1, :] = at
        parts.append(hot(centred == at))
    placed = contract(
        jnp.concatenate(parts, axis=1), jnp.concatenate(data, axis=0).astype(jnp.bfloat16), 1, 0
    ).astype(jnp.bfloat16)
    own_ref[...] = placed
    near_ref[...] = jnp.where(core_ref[0] == 0, placed[half:], placed[:half])
    far_ref[...] = jnp.where(core_ref[0] == 0, placed[:half], placed[half:])


def place_table(at_ref, rows):
    centred = (iota((rows, LANES), 0) - rows // 2).astype(jnp.float32)
    parts = [
        jnp.where(centred == at_ref[g : g + 1, :], 1.0, 0.0) for g in range(at_ref.shape[0])
    ]
    return jnp.concatenate(parts, axis=1)


def pick_kernel(
    core_ref,
    near_hbm,
    far_hbm,
    own_hbm,
    table_hbm,
    out_hbm,
    done_ref,
    near_ref,
    far_ref,
    own_ref,
    table_ref,
    out_ref,
    sems,
):
    done_ref[...] = jnp.zeros_like(done_ref)
    copies = fetch(
        [near_hbm, far_hbm, own_hbm, table_hbm], [near_ref, far_ref, own_ref, table_ref], sems
    )
    for copy in copies:
        copy.wait()
    half = near_ref.shape[0]
    near = near_ref[...].astype(jnp.float32)
    far = far_ref[...].astype(jnp.float32)
    own = jnp.concatenate(
        [
            own_ref[:half, :] + jnp.where(core_ref[0] == 0, far, near),
            own_ref[half:, :] + jnp.where(core_ref[0] == 0, near, far),
        ],
        axis=0,
    ).astype(jnp.bfloat16)
    stores = []
    parts = 4
    part = out_ref.shape[0] // parts
    for i in range(parts):
        rows = pl.ds(i * part, part)
        out_ref[rows, :] = contract(table_ref[rows, :], own, 1, 0).astype(jnp.bfloat16)
        stores += fetch([out_ref.at[rows, :]], [out_hbm.at[rows, :]], sems, 4 + i)
    for store in stores:
        store.wait()


def restore_kernel(table_ref, got_ref, out_ref):
    out_ref[...] = contract(table_ref[...], got_ref[...], 1, 0).astype(jnp.bfloat16)


def forward_kernel(
    core_ref,
    at_ref,
    own_ref,
    near_ref,
    far_ref,
    w_hbm,
    w_kv_t_hbm,
    query_hbm,
    kv_hbm,
    key_t_hbm,
    attn_t_hbm,
    probs_hbm,
    points_t_hbm,
    table_hbm,
    points_ref,
    w_ref,
    w_kv_t_ref,
    query_ref,
    kv_ref,
    key_t_ref,
    attn_t_ref,
    probs_ref,
    points_t_ref,
    table_ref,
    sems,
):
    width = w_ref.shape[0]
    head_dim = width // HEADS
    half = points_ref.shape[0] // 4
    copies = fetch([w_hbm, w_kv_t_hbm], [w_ref, w_kv_t_ref], sems)
    near, far = (near_ref[...], far_ref[...])
    points_ref[:half, :] = jnp.where(core_ref[0] == 0, far, near)
    points_ref[half : 3 * half, :] = own_ref[...]
    points_ref[3 * half :, :] = jnp.where(core_ref[0] == 0, near, far)
    table_ref[...] = place_table(at_ref, 2 * half).T.astype(jnp.bfloat16)
    stores = fetch([table_ref], [table_hbm], sems, 6)
    for copy in copies:
        copy.wait()
    points = points_ref[...]
    query_ref[...] = contract(points[half : 3 * half], w_ref[:, :width], 1, 0).astype(jnp.bfloat16)
    kv_ref[...] = contract(points, w_ref[:, width:], 1, 0).astype(jnp.bfloat16)
    kv_t = contract(w_kv_t_ref[...], points, 1, 1).astype(jnp.bfloat16)
    key_t_ref[...] = kv_t[:width]
    points_t_ref[...] = points.astype(jnp.float32).T.astype(jnp.bfloat16)
    stores += fetch(
        [query_ref, kv_ref, key_t_ref, points_t_ref],
        [query_hbm, kv_hbm, key_t_hbm, points_t_hbm],
        sems,
        7,
    )
    side = iota((1, LANES), 1) // head_dim
    factor = math.log2(math.e) / math.sqrt(head_dim)
    for head in range(HEADS):
        first = head * head_dim // LANES * LANES
        within = head * head_dim % LANES // head_dim
        query = query_ref[:, first : first + LANES]
        query = jnp.where(side == within, query, jnp.zeros_like(query))
        key = kv_ref[:, first : first + LANES]
        scores = jnp.concatenate(
            [
                contract(key[: 2 * half], query[:half], 1, 1),
                contract(key[2 * half :], query[half:], 1, 1),
            ],
            axis=1,
        )
        top = jnp.max(scores, axis=0, keepdims=True)
        weight = jnp.exp2((scores - top) * factor)
        probs = weight * (1.0 / jnp.sum(weight, axis=0, keepdims=True))
        probs_low = probs.astype(jnp.bfloat16)
        probs_ref[head] = probs_low
        stores += fetch([probs_ref.at[head]], [probs_hbm.at[head]], sems, 12 + head)
        value_t = kv_t[width + head * head_dim : width + (head + 1) * head_dim]
        attn_t_ref[head * head_dim : (head + 1) * head_dim, :] = jnp.concatenate(
            [
                contract(value_t[:, : 2 * half], probs_low[:, :half], 1, 0),
                contract(value_t[:, 2 * half :], probs_low[:, half:], 1, 0),
            ],
            axis=1,
        ).astype(jnp.bfloat16)
    stores += fetch([attn_t_ref], [attn_t_hbm], sems, 11)
    for store in stores:
        store.wait()


def weights(points_t, attn_t, grad_query, grad_kv, grads):
    half = grads.shape[0] // 2
    return (
        contract(points_t[:, half : 3 * half], grad_query, 1, 0),
        contract(points_t, grad_kv, 1, 0),
        contract(attn_t, grads, 1, 0),
    )


def backward_kernel(
    core_ref,
    at_ref,
    got_hbm,
    w_out_hbm,
    query_hbm,
    kv_hbm,
    key_t_hbm,
    attn_t_hbm,
    points_t_hbm,
    w_hbm,
    probs_hbm,
    send_hbm,
    keep_hbm,
    own_hbm,
    near_hbm,
    far_hbm,
    got_ref,
    w_out_ref,
    query_ref,
    kv_ref,
    key_t_ref,
    attn_t_ref,
    points_t_ref,
    w_ref,
    probs_ref,
    grad_query_ref,
    grad_kv_ref,
    query_t_ref,
    send_ref,
    keep_ref,
    own_ref,
    near_ref,
    far_ref,
    sems,
):
    width = w_out_ref.shape[0]
    head_dim = width // HEADS
    half = query_ref.shape[0] // 2
    scale = 1.0 / math.sqrt(head_dim)
    first_copies = fetch([got_hbm, w_out_hbm], [got_ref, w_out_ref], sems)
    copies = fetch(
        [attn_t_hbm, query_hbm, kv_hbm, key_t_hbm],
        [attn_t_ref, query_ref, kv_ref, key_t_ref],
        sems,
        2,
    )

    def fetch_probs(first, last):
        heads = range(first, min(last, HEADS))
        return fetch(
            [probs_hbm.at[h] for h in heads], [probs_ref.at[h] for h in heads], sems, 8 + first
        )

    per = LANES // head_dim
    probs_copies = fetch_probs(0, per)
    table = place_table(at_ref, 2 * half).astype(jnp.bfloat16)
    first_copies[0].wait()
    grads = contract(table, got_ref[...], 1, 0).astype(jnp.bfloat16)
    first_copies[1].wait()
    grad_attn = contract(grads, w_out_ref[...], 1, 1).astype(jnp.bfloat16)
    grad_attn_t = contract(w_out_ref[...], grads, 1, 1).astype(jnp.bfloat16)
    for copy in copies:
        copy.wait()
    side = iota((1, LANES), 1) // head_dim
    sides = ((slice(0, half), slice(0, 2 * half)), (slice(half, 2 * half), slice(2 * half, 4 * half)))
    for first in range(0, width, LANES):
        cols = slice(first, first + LANES)
        value_cols = slice(width + first, width + first + LANES)
        grad = grad_attn[:, cols]
        query = query_ref[:, cols]
        for copy in probs_copies:
            copy.wait()
        probs_copies = fetch_probs(first // head_dim + per, first // head_dim + 2 * per)
        if first == 0:
            late = fetch([points_t_hbm, w_hbm], [points_t_ref, w_ref], sems, 6)
        for mine, patch in sides:
            value = kv_ref[patch, value_cols]
            grad_key = jnp.zeros((2 * half, LANES), jnp.float32)
            grad_value = grad_key
            for within in range(LANES // head_dim):
                chans = slice(first + within * head_dim, first + (within + 1) * head_dim)
                probs = probs_ref[first // head_dim + within][:, mine]
                delta = jnp.sum(
                    grad_attn_t[chans, mine].astype(jnp.float32)
                    * attn_t_ref[chans, mine].astype(jnp.float32),
                    axis=0,
                    keepdims=True,
                )
                masked = jnp.where(side == within, grad[mine], jnp.zeros_like(grad[mine]))
                grad_probs = contract(value, masked, 1, 1)
                grad_scores = (probs.astype(jnp.float32) * (grad_probs - delta)).astype(jnp.bfloat16)
                grad_value = jnp.where(
                    side == within, contract(probs, grad[mine], 1, 0), grad_value
                )
                grad_key = jnp.where(
                    side == within, contract(grad_scores, query[mine], 1, 0), grad_key
                )
                query_t_ref[chans, mine] = (
                    contract(key_t_ref[chans, patch], grad_scores, 1, 0) * scale
                )
            grad_kv_ref[patch, cols] = (grad_key * scale).astype(jnp.bfloat16)
            grad_kv_ref[patch, value_cols] = grad_value.astype(jnp.bfloat16)
    grad_query_ref[...] = query_t_ref[...].T.astype(jnp.bfloat16)
    for copy in late:
        copy.wait()
    w_kv = w_ref[:, width:]
    own_ref[...] = contract(grad_query_ref[...], w_ref[:, :width], 1, 1) + contract(
        grad_kv_ref[half : 3 * half, :], w_kv, 1, 1
    )
    stores = fetch([own_ref], [own_hbm], sems, 8 + HEADS)
    before = contract(grad_kv_ref[:half, :], w_kv, 1, 1).astype(jnp.bfloat16)
    after = contract(grad_kv_ref[3 * half :, :], w_kv, 1, 1).astype(jnp.bfloat16)
    near_ref[...] = jnp.where(core_ref[0] == 0, after, before)
    far_ref[...] = jnp.where(core_ref[0] == 0, before, after)
    stores += fetch([near_ref, far_ref], [near_hbm, far_hbm], sems, 9 + HEADS)
    rows = width // 2
    for index, (side, out_ref, out_hbm) in enumerate(
        ((core_ref[0], keep_ref, keep_hbm), (1 - core_ref[0], send_ref, send_hbm))
    ):
        from_row = pl.multiple_of(side * rows, rows)
        of_query, of_kv, of_out = weights(
            points_t_ref[pl.ds(from_row, rows), :],
            attn_t_ref[pl.ds(from_row, rows), :],
            grad_query_ref[...],
            grad_kv_ref[...],
            grads,
        )
        out_ref[:, :width] = of_query.astype(out_ref.dtype)
        out_ref[:, width : 3 * width] = of_kv.astype(out_ref.dtype)
        out_ref[:, 3 * width :] = of_out.astype(out_ref.dtype)
        stores += fetch([out_ref], [out_hbm], sems, 11 + HEADS + index)
    for store in stores:
        store.wait()


def exchange(blocks):
    return lax.all_to_all(blocks, "curve", split_axis=0, concat_axis=0, tiled=True)


def swap(block, axis, mask):
    size = lax.axis_size(axis)
    return lax.ppermute(block, axis, [(i, i ^ mask) for i in range(size)])


def order_blocks(blocks, place):
    count = blocks.shape[0]
    tail = blocks.shape[1:]
    bit = 1
    while bit < count:
        pairs = blocks.reshape(count // (2 * bit), 2, bit, *tail)
        blocks = jnp.where((place & bit) != 0, pairs[:, ::-1], pairs).reshape(count, *tail)
        bit *= 2
    return blocks


def part_rows(total, side, keep_ref, send_ref):
    half = keep_ref.shape[0]
    keep_ref[...] = jnp.where(side == 0, total[:half], total[half:])
    send_ref[...] = jnp.where(side == 0, total[half:], total[:half]).astype(jnp.bfloat16)


def first_sum_kernel(
    sides_ref, kept_hbm, got_ref, keep_a, send_a, keep_b, send_b, kept_ref, sems
):
    half = kept_ref.shape[0] // 2
    parts = [pl.ds(0, half), pl.ds(half, half)]
    copies = fetch([kept_hbm.at[p, :] for p in parts], [kept_ref.at[p, :] for p in parts], sems)
    for index, (part, keep, send) in enumerate(
        zip(parts, (keep_a, keep_b), (send_a, send_b), strict=True)
    ):
        copies[index].wait()
        total = kept_ref[part, :].astype(jnp.float32) + got_ref[part, :].astype(jnp.float32)
        part_rows(total, sides_ref[index], keep, send)


def second_sum_kernel(
    sides_ref, kept_a_ref, got_a_ref, kept_b_ref, got_b_ref, keep_a, send_a, keep_b, send_b
):
    part_rows(
        kept_a_ref[...] + got_a_ref[...].astype(jnp.float32), sides_ref[1], keep_a, send_a
    )
    part_rows(
        kept_b_ref[...] + got_b_ref[...].astype(jnp.float32), sides_ref[0], keep_b, send_b
    )


def third_sum_kernel(
    line_ref, kept_a_ref, got_a_ref, kept_b_ref, got_b_ref, mine_ref, *refs
):
    sends, total_ref = (refs[:-1], refs[-1])
    rows = mine_ref.shape[0] // 2
    half = kept_a_ref.shape[0]
    total_ref[:half, :] = kept_a_ref[...] + got_a_ref[...].astype(jnp.float32)
    total_ref[half:, :] = kept_b_ref[...] + got_b_ref[...].astype(jnp.float32)
    for distance, out_ref in enumerate((mine_ref, *sends)):
        at = pl.multiple_of((line_ref[0] ^ distance) * rows, rows)
        out_ref[...] = jnp.concatenate(
            [total_ref[pl.ds(at, rows), :], total_ref[pl.ds(half + at, rows), :]], axis=0
        ).astype(out_ref.dtype)


def fourth_sum_kernel(mine_ref, *refs):
    others, out_ref = (refs[:-2], refs[-1])
    total = mine_ref[...]
    for other in others:
        total = total + other[...].astype(jnp.float32)
    out_ref[...] = total.astype(jnp.bfloat16)


def join_kernel(*refs):
    blocks, out_ref = (refs[:-1], refs[-1])
    rows = blocks[0].shape[0] // 2
    values = [block[...].astype(jnp.float32) for block in blocks]
    halves = [x[:rows] for x in values] + [x[rows:] for x in values]
    out_ref[...] = jnp.concatenate(halves, axis=0).astype(jnp.bfloat16)


def spread_kernel(n_line, place_ref, *refs):
    pieces, qkv_ref, out_ref = (refs[:-2], refs[-2], refs[-1])
    n_qkv = qkv_ref.shape[1]
    core, side_x, side_y, line = (place_ref[i] for i in range(4))
    rows = qkv_ref.shape[0] // (16 * n_line)
    for index, piece in enumerate(pieces):
        far_core, which = divmod(index, 5)
        far_x, far_y = ((0, 0), (1, 0), (0, 1), (1, 1), (1, 1))[which]
        near_x, near_y = (side_x ^ far_x, side_y ^ far_y)
        values = piece[...].astype(jnp.float32)
        for block in range(piece.shape[0] // rows):
            part, distance = divmod(block, n_line)
            if which == 4:
                part = 1
            first, second = ((near_x, near_y), (near_y, near_x))[part]
            unit = ((((core ^ far_core) * 2 + part) * 2 + first) * 2 + second) * n_line
            row = pl.multiple_of((unit + (line ^ distance)) * rows, rows)
            data = values[block * rows : (block + 1) * rows]
            qkv_ref[pl.ds(row, rows), :] = data[:, :n_qkv]
            out_ref[pl.ds(row, rows), :] = data[:, n_qkv:]


def sum_start(keep, send, sides, ready):
    n_line = lax.axis_size("curve") // 4
    line = lax.axis_index("curve") >> 2
    rows, width = keep.shape
    scalar = [SMEM] + [VMEM] * 4
    kept_a, send_a, kept_b, send_b = call(
        first_sum_kernel,
        [wide(rows // 4, width), low(rows // 4, width)] * 2,
        [sides, keep, swap(send, "curve", 1)],
        rows * width,
        [SMEM, HBM, VMEM],
        scratch=[space(keep), pltpu.SemaphoreType.DMA((2,))],
    )
    got_a = swap(send_a, "curve", 2)
    got_b = swap(send_b, "dp", 1)
    kept_a, send_a, kept_b, send_b = call(
        second_sum_kernel,
        [wide(rows // 8, width), low(rows // 8, width)] * 2,
        [sides, kept_a, got_a, kept_b, got_b],
        rows * width // 2,
        scalar,
    )
    got_a = swap(send_a, "dp", 1)
    got_b = swap(send_b, "curve", 2)
    rows = kept_a.shape[0] // n_line
    if rows % 8 == 0:
        mine, *sends = call(
            third_sum_kernel,
            [wide(2 * rows, width)] + [low(2 * rows, width)] * (n_line - 1),
            [line.reshape(1), kept_a, got_a, kept_b, got_b],
            kept_a.size,
            scalar,
            scratch=[pltpu.VMEM((2 * n_line * rows, width), jnp.float32)],
        )
    else:
        part_a = (kept_a + got_a.astype(jnp.float32)).reshape(n_line, rows, width)
        part_b = (kept_b + got_b.astype(jnp.float32)).reshape(n_line, rows, width)
        both = jnp.concatenate([part_a, part_b], axis=1)
        mine, *sends = [
            lax.dynamic_index_in_dim(both, line ^ k, 0, keepdims=False) for k in range(n_line)
        ]
        sends = [block.astype(jnp.bfloat16) for block in sends]
    others = [swap(block, "curve", 4 * (k + 1)) for k, block in enumerate(sends)]
    (mine,) = call(
        fourth_sum_kernel,
        [low(2 * rows, width)],
        [mine, *others, ready],
        mine.size,
        [VMEM] * n_line + [ANY],
    )
    blocks = [mine] + [swap(mine, "curve", 4 * k) for k in range(1, n_line)]
    if rows % 8 == 0:
        (own,) = call(join_kernel, [low(2 * n_line * rows, width)], blocks, mine.size)
    else:
        blocks = order_blocks(jnp.stack(blocks), line)
        own = jnp.swapaxes(blocks.reshape(n_line, 2, rows, width), 0, 1)
        own = own.reshape(2 * n_line * rows, width)
        line = jnp.zeros_like(line)
    return (own, line)


def sum_finish(own, line, sides, width_qkv):
    n_line = lax.axis_size("curve") // 4
    core = lax.axis_index("curve") & 1
    half, width = (own.shape[0] // 2, own.shape[1])
    over_x = swap(own, "curve", 2)
    over_y = swap(own, "dp", 1)
    pieces = [own, over_x, over_y, swap(over_y[:half], "curve", 2), swap(over_x[half:], "dp", 1)]
    pieces += [swap(piece, "curve", 1) for piece in pieces]
    return call(
        functools.partial(spread_kernel, n_line),
        [wide(16 * half, width_qkv), wide(16 * half, width - width_qkv)],
        [jnp.stack([core, sides[0], sides[1], line]), *pieces],
        SPREAD_FLOPS,
        [SMEM] + [VMEM] * len(pieces),
    )


def halo(near, far):
    size = lax.axis_size("curve")
    route = [(i, (i + 2 * (i % 2) - 1) % size) for i in range(size)]
    return (swap(near, "curve", 1), lax.ppermute(far, "curve", route))


def on_device(points, grad_out, dest_dev, dest_row, w_qkv, w_out):
    rows, width = points.shape[1:]
    half = rows - PATCH // 2
    n_dev = lax.axis_size("curve")
    cap = 2 * rows // n_dev
    total = n_dev * cap
    place_flops = 2 * total * rows * width
    me = lax.axis_index("curve")
    core = (me & 1).reshape(1)
    sides = jnp.stack([(me >> 1) & 1, lax.axis_index("dp")])
    ids = jax.ShapeDtypeStruct((1, rows), jnp.int32)
    send_points, slots = call(
        pack_points_kernel,
        [low(n_dev, cap * width // LANES + INFO_ROWS, LANES), ids],
        [dest_dev, dest_row, points[0]],
        place_flops,
        [HBM] * 3,
        scratch=[space(ids), space(ids), space(low(rows, width)), pltpu.SemaphoreType.DMA((3,))],
        mib=60,
    )
    got_points = exchange(send_points)
    send_grads, restore_table = call(
        pack_grads_kernel, [low(total, width), low(rows, total)], [slots, grad_out[0]], place_flops
    )
    own, near, far, at = call(
        place_points_kernel,
        [
            low(rows, width),
            low(half, width),
            low(half, width),
            wide(total // LANES, LANES),
        ],
        [core, got_points],
        place_flops,
        [SMEM, VMEM],
    )
    near, far = halo(near, far)
    send_grads = gate(send_grads, at, flops=GATE_FLOPS)
    got_grads = exchange(send_grads.reshape(n_dev, cap, width)).reshape(total, width)
    saved = [
        low(rows, width),
        low(2 * rows, 2 * width),
        low(width, 2 * rows),
        low(width, rows),
        low(HEADS, PATCH, PATCH),
        low(width, 2 * rows),
        low(total, rows),
    ]
    query, kv, key_t, attn_t, probs, points_t, pick_table = call(
        forward_kernel,
        saved,
        [core, at, own, near, far, w_qkv, w_qkv[:, width:].T],
        FORWARD_FLOPS,
        [SMEM] + [VMEM] * 4 + [HBM] * 2,
        [HBM] * len(saved),
        [space(low(2 * rows, width)), space(low(width, 3 * width)), space(low(2 * width, width))]
        + [space(x) for x in saved]
        + [pltpu.SemaphoreType.DMA((12 + HEADS,))],
        60,
    )
    held = [got_grads, w_out, query, kv, key_t, attn_t, points_t, w_qkv, probs]
    made = [
        low(width // 2, 4 * width),
        low(width // 2, 4 * width),
        wide(rows, width),
        low(half, width),
        low(half, width),
    ]
    send, keep, own_input, near, far = call(
        backward_kernel,
        made,
        [core, at, *held],
        32 * rows * rows * width + 22 * rows * width * width,
        [SMEM, VMEM] + [HBM] * len(held),
        [HBM] * len(made),
        [space(x) for x in held]
        + [space(low(rows, width)), space(low(2 * rows, 2 * width)), space(wide(width, rows))]
        + [space(x) for x in made]
        + [pltpu.SemaphoreType.DMA((13 + HEADS,))],
        63,
    )
    near, far = halo(near, far)
    picked = low(total, width)
    picked, done = call(
        pick_kernel,
        [picked, wide(8, LANES)],
        [core, near, far, own_input, pick_table],
        place_flops,
        [SMEM] + [HBM] * 4,
        [HBM, VMEM],
        [space(x) for x in (near, far, own_input, pick_table, picked)] + [pltpu.SemaphoreType.DMA((8,))],
        63,
    )
    gathered, line = sum_start(keep, send, sides, done)
    picked = gate(picked, gathered, flops=GATE_FLOPS)
    returned = exchange(picked.reshape(n_dev, cap, width)).reshape(total, width)
    weight_qkv, weight_out = sum_finish(gathered, line, sides, 3 * width)
    (result,) = call(restore_kernel, [low(rows, width)], [restore_table, returned], place_flops)
    return (result[None], weight_qkv, weight_out)


def solution(mesh):
    placed = (
        P("dp", "curve", None),
        P("dp", "curve", None),
        P("dp", "curve"),
        P("dp", "curve"),
        P(),
        P(),
    )
    return jax.shard_map(
        on_device,
        mesh=mesh,
        in_specs=placed,
        out_specs=(P("dp", "curve", None), P(), P()),
        check_vma=False,
    )
```

```python
import functools
import math

import jax
import jax.numpy as jnp
from jax import lax
from jax.experimental import pallas as pl
from jax.experimental.pallas import tpu as pltpu
from jax.sharding import PartitionSpec as P

HEADS = 8
PATCH = 512
INFO_ROWS = 8
GATE_FLOPS = 10**10
FORWARD_FLOPS = 10**11
SPREAD_FLOPS = 13 * 10**9
LANES = 128


def contract(left, right, left_dim, right_dim):
    return lax.dot_general(
        left, right, (((left_dim,), (right_dim,)), ((), ())), preferred_element_type=jnp.float32
    )


def iota(shape, dim):
    return lax.broadcasted_iota(jnp.int32, shape, dim)


def hot(mask):
    return jnp.where(mask, 1.0, 0.0).astype(jnp.bfloat16)


VMEM = pl.BlockSpec(memory_space=pltpu.VMEM)
SMEM = pl.BlockSpec(memory_space=pltpu.SMEM)
HBM = pl.BlockSpec(memory_space=pltpu.HBM)
ANY = pl.BlockSpec(memory_space=pl.ANY)


def low(*shape):
    return jax.ShapeDtypeStruct(shape, jnp.bfloat16)


def wide(*shape):
    return jax.ShapeDtypeStruct(shape, jnp.float32)


def space(shape):
    return pltpu.VMEM(shape.shape, shape.dtype)


def call(kernel, outs, args, flops, ins=None, out_specs=None, scratch=(), mib=16):
    moved = sum(math.prod(x.shape) * x.dtype.itemsize for x in (*outs, *args))
    return pl.pallas_call(
        kernel,
        out_shape=outs,
        in_specs=ins or [VMEM] * len(args),
        out_specs=out_specs or [VMEM] * len(outs),
        scratch_shapes=list(scratch),
        compiler_params=pltpu.CompilerParams(vmem_limit_bytes=mib * 2**20),
        cost_estimate=pl.CostEstimate(flops=flops, bytes_accessed=moved, transcendentals=0),
    )(*args)


def fetch(sources, places, sems, first=0):
    copies = [
        pltpu.make_async_copy(source, place, sems.at[first + i])
        for i, (source, place) in enumerate(zip(sources, places, strict=True))
    ]
    for copy in copies:
        copy.start()
    return copies


def gate(block, *others, flops=0):
    return pl.pallas_call(
        lambda *refs: None,
        out_shape=jax.ShapeDtypeStruct(block.shape, block.dtype),
        in_specs=[HBM] + [ANY] * len(others),
        out_specs=HBM,
        input_output_aliases={0: 0},
        cost_estimate=pl.CostEstimate(flops=flops, bytes_accessed=0, transcendentals=0),
    )(block, *others)


def pack_points_kernel(dev_hbm, row_hbm, x_hbm, out_ref, slots_ref, dev_ref, row_ref, x_ref, sems):
    copies = fetch([dev_hbm, row_hbm, x_hbm], [dev_ref, row_ref, x_ref], sems)
    n_dev, block, _ = out_ref.shape
    rows, width = x_ref.shape
    cap = (block - INFO_ROWS) * LANES // width
    copies[0].wait()
    dev = dev_ref[...]
    mine = iota((n_dev, rows), 0) == dev
    mine_f = jnp.where(mine, 1.0, 0.0)
    upto = hot(iota((rows, rows), 0) <= iota((rows, rows), 1))
    running = contract(mine_f.astype(jnp.bfloat16), upto, 1, 0)
    rank = (jnp.sum(running * mine_f, axis=0, keepdims=True) - 1.0).astype(jnp.int32)
    slots = dev * cap + rank
    slots_ref[...] = slots
    at_rank = hot(iota((LANES, rows), 0) % cap == rank)
    copies[1].wait()
    centred = (row_ref[...] - rows // 2).astype(jnp.float32)
    told = jnp.concatenate([mine_f * centred, mine_f], axis=0).astype(jnp.bfloat16)
    got = contract(told, at_rank, 1, 1)
    info = jnp.where(got[n_dev:] > 0.5, got[:n_dev], float(rows))
    per = 256 // cap
    copies[2].wait()
    for first in range(0, n_dev, per):
        pick = hot(iota((per * cap, rows), 0) + first * cap == slots)
        data = contract(pick, x_ref[...], 1, 0)
        for j in range(per):
            dest = first + j
            stack = [
                data[j * cap : (j + 1) * cap, col : col + LANES] for col in range(0, width, LANES)
            ]
            stack.append(jnp.broadcast_to(info[dest : dest + 1], (INFO_ROWS, LANES)))
            out_ref[dest] = jnp.concatenate(stack, axis=0).astype(jnp.bfloat16)


def pack_grads_kernel(slots_ref, x_ref, out_ref, back_ref):
    total = out_ref.shape[0]
    rows = x_ref.shape[0]
    pick = jnp.where(iota((total, rows), 0) == slots_ref[...], 1.0, 0.0)
    out_ref[...] = contract(pick.astype(jnp.bfloat16), x_ref[...], 1, 0).astype(jnp.bfloat16)
    back_ref[...] = pick.T.astype(jnp.bfloat16)


def place_points_kernel(core_ref, got_ref, near_ref, far_ref, at_ref):
    n_dev, block, _ = got_ref.shape
    rows, width = (2 * near_ref.shape[0], near_ref.shape[1])
    cap = (block - INFO_ROWS) * LANES // width
    half = rows // 2
    per = LANES // cap
    source = iota((1, LANES), 1) // cap
    centred = (iota((rows, LANES), 0) - half).astype(jnp.float32)
    parts, data = ([], [])
    for first in range(0, n_dev, per):
        at = jnp.zeros((1, LANES), jnp.float32)
        for j in range(per):
            got = got_ref[first + j]
            info = got.astype(jnp.float32)[block - INFO_ROWS : block - INFO_ROWS + 1]
            at = jnp.where(source == j, info, at)
            if cap % 16:
                got = got.astype(jnp.float32)
            cols = [got[i * cap : (i + 1) * cap] for i in range(width // LANES)]
            data.append(jnp.concatenate(cols, axis=1))
        at_ref[first // per : first // per + 1, :] = at
        parts.append(hot(centred == at))
    placed = contract(
        jnp.concatenate(parts, axis=1), jnp.concatenate(data, axis=0).astype(jnp.bfloat16), 1, 0
    ).astype(jnp.bfloat16)
    near_ref[...] = jnp.where(core_ref[0] == 0, placed[half:], placed[:half])
    far_ref[...] = jnp.where(core_ref[0] == 0, placed[:half], placed[half:])


def place_table(at_ref, rows):
    centred = (iota((rows, LANES), 0) - rows // 2).astype(jnp.float32)
    parts = [
        jnp.where(centred == at_ref[g : g + 1, :], 1.0, 0.0) for g in range(at_ref.shape[0])
    ]
    return jnp.concatenate(parts, axis=1)


def pick_kernel(
    core_ref,
    near_hbm,
    far_hbm,
    own_hbm,
    table_hbm,
    out_hbm,
    done_ref,
    near_ref,
    far_ref,
    own_ref,
    table_ref,
    out_ref,
    sems,
):
    done_ref[...] = jnp.zeros_like(done_ref)
    copies = fetch(
        [near_hbm, far_hbm, own_hbm, table_hbm], [near_ref, far_ref, own_ref, table_ref], sems
    )
    for copy in copies:
        copy.wait()
    half = near_ref.shape[0]
    near = near_ref[...].astype(jnp.float32)
    far = far_ref[...].astype(jnp.float32)
    own = jnp.concatenate(
        [
            own_ref[:half, :] + jnp.where(core_ref[0] == 0, far, near),
            own_ref[half:, :] + jnp.where(core_ref[0] == 0, near, far),
        ],
        axis=0,
    ).astype(jnp.bfloat16)
    stores = []
    parts = 4
    part = out_ref.shape[0] // parts
    for i in range(parts):
        rows = pl.ds(i * part, part)
        out_ref[rows, :] = contract(table_ref[rows, :], own, 1, 0).astype(jnp.bfloat16)
        stores += fetch([out_ref.at[rows, :]], [out_hbm.at[rows, :]], sems, 4 + i)
    for store in stores:
        store.wait()


def restore_kernel(table_ref, got_ref, out_ref):
    out_ref[...] = contract(table_ref[...], got_ref[...], 1, 0).astype(jnp.bfloat16)


def forward_kernel(
    core_ref,
    at_ref,
    near_sent_ref,
    far_sent_ref,
    near_ref,
    far_ref,
    w_hbm,
    w_kv_t_hbm,
    query_hbm,
    value_hbm,
    key_t_hbm,
    attn_t_hbm,
    probs_hbm,
    points_t_hbm,
    table_hbm,
    points_ref,
    w_ref,
    w_kv_t_ref,
    query_ref,
    value_ref,
    key_t_ref,
    attn_t_ref,
    probs_ref,
    points_t_ref,
    table_ref,
    sems,
):
    width = w_ref.shape[0]
    head_dim = width // HEADS
    half = points_ref.shape[0] // 4
    copies = fetch([w_hbm, w_kv_t_hbm], [w_ref, w_kv_t_ref], sems)
    even = core_ref[0] == 0
    quarters = ((far_ref, near_ref), (far_sent_ref, near_sent_ref))
    for i, (on_even, on_odd) in enumerate((*quarters, *(pair[::-1] for pair in quarters[::-1]))):
        points_ref[i * half : (i + 1) * half, :] = jnp.where(even, on_even[...], on_odd[...])
    table_ref[...] = place_table(at_ref, 2 * half).T.astype(jnp.bfloat16)
    stores = fetch([table_ref], [table_hbm], sems, 6)
    for copy in copies:
        copy.wait()
    points = points_ref[...]
    query_ref[...] = contract(points[half : 3 * half], w_ref[:, :width], 1, 0).astype(jnp.bfloat16)
    keys = contract(points, w_ref[:, width : 2 * width], 1, 0).astype(jnp.bfloat16)
    value_ref[...] = contract(points, w_ref[:, 2 * width :], 1, 0).astype(jnp.bfloat16)
    kv_t = contract(w_kv_t_ref[...], points, 1, 1).astype(jnp.bfloat16)
    key_t_ref[...] = kv_t[:width]
    points_t_ref[...] = points.astype(jnp.float32).T.astype(jnp.bfloat16)
    stores += fetch(
        [query_ref, value_ref, key_t_ref, points_t_ref],
        [query_hbm, value_hbm, key_t_hbm, points_t_hbm],
        sems,
        7,
    )
    side = iota((1, LANES), 1) // head_dim
    factor = math.log2(math.e) / math.sqrt(head_dim)
    for head in range(HEADS):
        first = head * head_dim // LANES * LANES
        within = head * head_dim % LANES // head_dim
        query = query_ref[:, first : first + LANES]
        query = jnp.where(side == within, query, jnp.zeros_like(query))
        key = keys[:, first : first + LANES]
        scores = jnp.concatenate(
            [
                contract(key[: 2 * half], query[:half], 1, 1),
                contract(key[2 * half :], query[half:], 1, 1),
            ],
            axis=1,
        )
        top = jnp.max(scores, axis=0, keepdims=True)
        weight = jnp.exp2((scores - top) * factor)
        probs = weight * (1.0 / jnp.sum(weight, axis=0, keepdims=True))
        probs_low = probs.astype(jnp.bfloat16)
        probs_ref[head] = probs_low
        stores += fetch([probs_ref.at[head]], [probs_hbm.at[head]], sems, 12 + head)
        value_t = kv_t[width + head * head_dim : width + (head + 1) * head_dim]
        attn_t_ref[head * head_dim : (head + 1) * head_dim, :] = jnp.concatenate(
            [
                contract(value_t[:, : 2 * half], probs_low[:, :half], 1, 0),
                contract(value_t[:, 2 * half :], probs_low[:, half:], 1, 0),
            ],
            axis=1,
        ).astype(jnp.bfloat16)
    stores += fetch([attn_t_ref], [attn_t_hbm], sems, 11)
    for store in stores:
        store.wait()


def weights(points_t, attn_t, grad_query, grad_kv, grads):
    half = grads.shape[0] // 2
    return (
        contract(points_t[:, half : 3 * half], grad_query, 1, 0),
        contract(points_t, grad_kv, 1, 0),
        contract(attn_t, grads, 1, 0),
    )


def backward_kernel(
    core_ref,
    at_ref,
    got_hbm,
    w_out_hbm,
    query_hbm,
    value_hbm,
    key_t_hbm,
    attn_t_hbm,
    points_t_hbm,
    w_hbm,
    probs_hbm,
    send_hbm,
    keep_hbm,
    own_hbm,
    near_hbm,
    far_hbm,
    got_ref,
    w_out_ref,
    query_ref,
    value_ref,
    key_t_ref,
    attn_t_ref,
    points_t_ref,
    w_ref,
    probs_ref,
    grad_query_ref,
    grad_kv_ref,
    query_t_ref,
    send_ref,
    keep_ref,
    own_ref,
    near_ref,
    far_ref,
    sems,
):
    width = w_out_ref.shape[0]
    head_dim = width // HEADS
    half = query_ref.shape[0] // 2
    scale = 1.0 / math.sqrt(head_dim)
    first_copies = fetch([got_hbm, w_out_hbm], [got_ref, w_out_ref], sems)
    copies = fetch(
        [attn_t_hbm, query_hbm, value_hbm, key_t_hbm],
        [attn_t_ref, query_ref, value_ref, key_t_ref],
        sems,
        2,
    )

    def fetch_probs(first, last):
        heads = range(first, min(last, HEADS))
        return fetch(
            [probs_hbm.at[h] for h in heads], [probs_ref.at[h] for h in heads], sems, 8 + first
        )

    per = LANES // head_dim
    probs_copies = fetch_probs(0, per)
    table = place_table(at_ref, 2 * half).astype(jnp.bfloat16)
    first_copies[0].wait()
    grads = contract(table, got_ref[...], 1, 0).astype(jnp.bfloat16)
    first_copies[1].wait()
    grad_attn = contract(grads, w_out_ref[...], 1, 1).astype(jnp.bfloat16)
    grad_attn_t = contract(w_out_ref[...], grads, 1, 1).astype(jnp.bfloat16)
    for copy in copies:
        copy.wait()
    side = iota((1, LANES), 1) // head_dim
    sides = ((slice(0, half), slice(0, 2 * half)), (slice(half, 2 * half), slice(2 * half, 4 * half)))
    for first in range(0, width, LANES):
        cols = slice(first, first + LANES)
        value_cols = slice(width + first, width + first + LANES)
        grad = grad_attn[:, cols]
        query = query_ref[:, cols]
        for copy in probs_copies:
            copy.wait()
        probs_copies = fetch_probs(first // head_dim + per, first // head_dim + 2 * per)
        if first == 0:
            late = fetch([points_t_hbm, w_hbm], [points_t_ref, w_ref], sems, 6)
        for mine, patch in sides:
            value = value_ref[patch, cols]
            grad_key = jnp.zeros((2 * half, LANES), jnp.float32)
            grad_value = grad_key
            for within in range(LANES // head_dim):
                chans = slice(first + within * head_dim, first + (within + 1) * head_dim)
                probs = probs_ref[first // head_dim + within][:, mine]
                delta = jnp.sum(
                    grad_attn_t[chans, mine].astype(jnp.float32)
                    * attn_t_ref[chans, mine].astype(jnp.float32),
                    axis=0,
                    keepdims=True,
                )
                masked = jnp.where(side == within, grad[mine], jnp.zeros_like(grad[mine]))
                grad_probs = contract(value, masked, 1, 1)
                grad_scores = (probs.astype(jnp.float32) * (grad_probs - delta)).astype(jnp.bfloat16)
                grad_value = jnp.where(
                    side == within, contract(probs, grad[mine], 1, 0), grad_value
                )
                grad_key = jnp.where(
                    side == within, contract(grad_scores, query[mine], 1, 0), grad_key
                )
                query_t_ref[chans, mine] = (
                    contract(key_t_ref[chans, patch], grad_scores, 1, 0) * scale
                )
            grad_kv_ref[patch, cols] = (grad_key * scale).astype(jnp.bfloat16)
            grad_kv_ref[patch, value_cols] = grad_value.astype(jnp.bfloat16)
    grad_query_ref[...] = query_t_ref[...].T.astype(jnp.bfloat16)
    for copy in late:
        copy.wait()
    w_kv = w_ref[:, width:]
    own_ref[...] = contract(grad_query_ref[...], w_ref[:, :width], 1, 1) + contract(
        grad_kv_ref[half : 3 * half, :], w_kv, 1, 1
    )
    stores = fetch([own_ref], [own_hbm], sems, 8 + HEADS)
    before = contract(grad_kv_ref[:half, :], w_kv, 1, 1).astype(jnp.bfloat16)
    after = contract(grad_kv_ref[3 * half :, :], w_kv, 1, 1).astype(jnp.bfloat16)
    near_ref[...] = jnp.where(core_ref[0] == 0, after, before)
    far_ref[...] = jnp.where(core_ref[0] == 0, before, after)
    stores += fetch([near_ref, far_ref], [near_hbm, far_hbm], sems, 9 + HEADS)
    rows = width // 2
    for index, (side, out_ref, out_hbm) in enumerate(
        ((core_ref[0], keep_ref, keep_hbm), (1 - core_ref[0], send_ref, send_hbm))
    ):
        from_row = pl.multiple_of(side * rows, rows)
        of_query, of_kv, of_out = weights(
            points_t_ref[pl.ds(from_row, rows), :],
            attn_t_ref[pl.ds(from_row, rows), :],
            grad_query_ref[...],
            grad_kv_ref[...],
            grads,
        )
        out_ref[:, :width] = of_query.astype(out_ref.dtype)
        out_ref[:, width : 3 * width] = of_kv.astype(out_ref.dtype)
        out_ref[:, 3 * width :] = of_out.astype(out_ref.dtype)
        stores += fetch([out_ref], [out_hbm], sems, 11 + HEADS + index)
    for store in stores:
        store.wait()


def exchange(blocks):
    return lax.all_to_all(blocks, "curve", split_axis=0, concat_axis=0, tiled=True)


def swap(block, axis, mask):
    size = lax.axis_size(axis)
    return lax.ppermute(block, axis, [(i, i ^ mask) for i in range(size)])


def order_blocks(blocks, place):
    count = blocks.shape[0]
    tail = blocks.shape[1:]
    bit = 1
    while bit < count:
        pairs = blocks.reshape(count // (2 * bit), 2, bit, *tail)
        blocks = jnp.where((place & bit) != 0, pairs[:, ::-1], pairs).reshape(count, *tail)
        bit *= 2
    return blocks


def first_sum_kernel(sides_ref, kept_ref, got_ref, keep, send_x, send_y, send_xy):
    rows = keep.shape[0]
    side_x, side_y = (sides_ref[0], sides_ref[1])
    quarters = []
    for far_x, far_y in ((1, 0), (1, 1), (0, 1), (0, 0)):
        at = ((side_x ^ far_x) * 2 + (side_y ^ far_y)) * rows
        quarters.append(pl.ds(pl.multiple_of(at, rows), rows))
    for quarter, out_ref in zip(quarters, (send_x, send_xy, send_y, keep), strict=True):
        total = kept_ref[quarter, :].astype(jnp.float32) + got_ref[quarter, :].astype(jnp.float32)
        out_ref[...] = total.astype(out_ref.dtype)


def second_sum_kernel(line_ref, kept_ref, *refs):
    got, mine_ref, sends, total_ref = (refs[:3], refs[3], refs[4:-1], refs[-1])
    rows = mine_ref.shape[0]
    total = kept_ref[...]
    for ref in got:
        total = total + ref[...].astype(jnp.float32)
    total_ref[...] = total
    for distance, out_ref in enumerate((mine_ref, *sends)):
        at = pl.multiple_of((line_ref[0] ^ distance) * rows, rows)
        out_ref[...] = total_ref[pl.ds(at, rows), :].astype(out_ref.dtype)


def third_sum_kernel(mine_ref, *refs):
    others, out_ref = (refs[:-2], refs[-1])
    total = mine_ref[...]
    for other in others:
        total = total + other[...].astype(jnp.float32)
    out_ref[...] = total.astype(jnp.bfloat16)


def join_kernel(*refs):
    refs[-1][...] = jnp.concatenate([ref[...] for ref in refs[:-1]], axis=0)


def spread_kernel(n_line, place_ref, *refs):
    pieces, qkv_ref, out_ref = (refs[:-2], refs[-2], refs[-1])
    n_qkv = qkv_ref.shape[1]
    core, side_x, side_y, line = (place_ref[i] for i in range(4))
    rows = pieces[0].shape[0] // n_line
    for index, piece in enumerate(pieces):
        near_x, near_y = (side_x ^ (index & 1), side_y ^ (index >> 1 & 1))
        quarter = ((core ^ (index >> 2)) * 2 + near_x) * 2 + near_y
        for distance in range(n_line):
            row = pl.multiple_of((quarter * n_line + (line ^ distance)) * rows, rows)
            data = piece[distance * rows : (distance + 1) * rows, :].astype(jnp.float32)
            qkv_ref[pl.ds(row, rows), :] = data[:, :n_qkv]
            out_ref[pl.ds(row, rows), :] = data[:, n_qkv:]


def swap_across(block):
    size = lax.axis_size("curve")
    route = [(2 * i + j, 2 * (i ^ 2) + (j ^ 1)) for i in range(size) for j in range(2)]
    return lax.ppermute(block, ("curve", "dp"), route)


def sum_start(keep, send, sides):
    n_line = lax.axis_size("curve") // 4
    line = lax.axis_index("curve") >> 2
    rows, width = keep.shape
    rows = rows // 4
    kept, send_x, send_y, send_xy = call(
        first_sum_kernel,
        [wide(rows, width)] + [low(rows, width)] * 3,
        [sides, keep, swap(send, "curve", 1)],
        4 * rows * width,
        [SMEM, VMEM, VMEM],
    )
    got = [swap(send_x, "curve", 2), swap(send_y, "dp", 1), swap_across(send_xy)]
    rows = rows // n_line
    if rows % 16 == 0:
        mine, *sends = call(
            second_sum_kernel,
            [wide(rows, width)] + [low(rows, width)] * (n_line - 1),
            [line.reshape(1), kept, *got],
            kept.size,
            [SMEM] + [VMEM] * 4,
            scratch=[space(kept)],
        )
        return (mine, sends)
    total = kept + sum(x.astype(jnp.float32) for x in got)
    total = total.reshape(n_line, rows, width)
    mine, *sends = [
        lax.dynamic_index_in_dim(total, line ^ k, 0, keepdims=False) for k in range(n_line)
    ]
    return (mine, [block.astype(jnp.bfloat16) for block in sends])


def sum_line(mine, sends, ready):
    n_line = len(sends) + 1
    line = lax.axis_index("curve") >> 2
    rows, width = mine.shape
    others = [swap(block, "curve", 4 * (k + 1)) for k, block in enumerate(sends)]
    (mine,) = call(third_sum_kernel, [low(rows, width)], [mine, *others, ready], mine.size)
    blocks = [mine] + [swap(mine, "curve", 4 * k) for k in range(1, n_line)]
    if rows % 16 == 0:
        (own,) = call(join_kernel, [low(n_line * rows, width)], blocks, mine.size)
        return (own, line, n_line)
    own = order_blocks(jnp.stack(blocks), line).reshape(n_line * rows, width)
    return (own, jnp.zeros_like(line), 1)


def sum_finish(own, line, n_line, sides, width_qkv):
    core = lax.axis_index("curve") & 1
    rows, width = own.shape
    over_x = swap(own, "curve", 2)
    pieces = [own, over_x, swap(own, "dp", 1), swap(over_x, "dp", 1)]
    pieces += [swap(piece, "curve", 1) for piece in pieces]
    return call(
        functools.partial(spread_kernel, n_line),
        [wide(8 * rows, width_qkv), wide(8 * rows, width - width_qkv)],
        [jnp.stack([core, sides[0], sides[1], line]), *pieces],
        SPREAD_FLOPS,
        [SMEM] + [VMEM] * len(pieces),
    )


def halo(near, far):
    size = lax.axis_size("curve")
    route = [(i, (i + 2 * (i % 2) - 1) % size) for i in range(size)]
    return (swap(near, "curve", 1), lax.ppermute(far, "curve", route))


def on_device(points, grad_out, dest_dev, dest_row, w_qkv, w_out):
    rows, width = points.shape[1:]
    half = rows - PATCH // 2
    n_dev = lax.axis_size("curve")
    cap = 2 * rows // n_dev
    total = n_dev * cap
    place_flops = 2 * total * rows * width
    me = lax.axis_index("curve")
    core = (me & 1).reshape(1)
    sides = jnp.stack([(me >> 1) & 1, lax.axis_index("dp")])
    ids = jax.ShapeDtypeStruct((1, rows), jnp.int32)
    send_points, slots = call(
        pack_points_kernel,
        [low(n_dev, cap * width // LANES + INFO_ROWS, LANES), ids],
        [dest_dev, dest_row, points[0]],
        place_flops,
        [HBM] * 3,
        scratch=[space(ids), space(ids), space(low(rows, width)), pltpu.SemaphoreType.DMA((3,))],
        mib=60,
    )
    got_points = exchange(send_points)
    send_grads, restore_table = call(
        pack_grads_kernel, [low(total, width), low(rows, total)], [slots, grad_out[0]], place_flops
    )
    near_sent, far_sent, at = call(
        place_points_kernel,
        [
            low(half, width),
            low(half, width),
            wide(total // LANES, LANES),
        ],
        [core, got_points],
        place_flops,
        [SMEM, VMEM],
    )
    near, far = halo(near_sent, far_sent)
    send_grads = gate(send_grads, at, flops=GATE_FLOPS)
    got_grads = exchange(send_grads.reshape(n_dev, cap, width)).reshape(total, width)
    saved = [
        low(rows, width),
        low(2 * rows, width),
        low(width, 2 * rows),
        low(width, rows),
        low(HEADS, PATCH, PATCH),
        low(width, 2 * rows),
        low(total, rows),
    ]
    query, value, key_t, attn_t, probs, points_t, pick_table = call(
        forward_kernel,
        saved,
        [core, at, near_sent, far_sent, near, far, w_qkv, w_qkv[:, width:].T],
        FORWARD_FLOPS,
        [SMEM] + [VMEM] * 5 + [HBM] * 2,
        [HBM] * len(saved),
        [space(low(2 * rows, width)), space(low(width, 3 * width)), space(low(2 * width, width))]
        + [space(x) for x in saved]
        + [pltpu.SemaphoreType.DMA((12 + HEADS,))],
        60,
    )
    held = [got_grads, w_out, query, value, key_t, attn_t, points_t, w_qkv, probs]
    made = [
        low(width // 2, 4 * width),
        low(width // 2, 4 * width),
        wide(rows, width),
        low(half, width),
        low(half, width),
    ]
    send, keep, own_input, near, far = call(
        backward_kernel,
        made,
        [core, at, *held],
        32 * rows * rows * width + 22 * rows * width * width,
        [SMEM, VMEM] + [HBM] * len(held),
        [HBM] * len(made),
        [space(x) for x in held]
        + [space(low(rows, width)), space(low(2 * rows, 2 * width)), space(wide(width, rows))]
        + [space(x) for x in made]
        + [pltpu.SemaphoreType.DMA((13 + HEADS,))],
        63,
    )
    mine, sends = sum_start(keep, send, sides)
    near, far = halo(near, far)
    picked = low(total, width)
    picked, done = call(
        pick_kernel,
        [picked, wide(8, LANES)],
        [core, near, far, own_input, pick_table],
        place_flops,
        [SMEM] + [HBM] * 4,
        [HBM, VMEM],
        [space(x) for x in (near, far, own_input, pick_table, picked)] + [pltpu.SemaphoreType.DMA((8,))],
        63,
    )
    gathered, line, n_line = sum_line(mine, sends, done)
    picked = gate(picked, gathered, flops=GATE_FLOPS)
    returned = exchange(picked.reshape(n_dev, cap, width)).reshape(total, width)
    weight_qkv, weight_out = sum_finish(gathered, line, n_line, sides, 3 * width)
    (result,) = call(restore_kernel, [low(rows, width)], [restore_table, returned], place_flops)
    return (result[None], weight_qkv, weight_out)


def solution(mesh):
    placed = (
        P("dp", "curve", None),
        P("dp", "curve", None),
        P("dp", "curve"),
        P("dp", "curve"),
        P(),
        P(),
    )
    return jax.shard_map(
        on_device,
        mesh=mesh,
        in_specs=placed,
        out_specs=(P("dp", "curve", None), P(), P()),
        check_vma=False,
    )
```

```python
import functools
import math

import jax
import jax.numpy as jnp
from jax import lax
from jax.experimental import pallas as pl
from jax.experimental.pallas import tpu as pltpu
from jax.sharding import PartitionSpec as P

HEADS = 8
PATCH = 512
INFO_ROWS = 8
GATE_FLOPS = 10**10
FORWARD_FLOPS = 10**11
SPREAD_FLOPS = 13 * 10**9
LANES = 128


def contract(left, right, left_dim, right_dim):
    return lax.dot_general(
        left, right, (((left_dim,), (right_dim,)), ((), ())), preferred_element_type=jnp.float32
    )


def iota(shape, dim):
    return lax.broadcasted_iota(jnp.int32, shape, dim)


def hot(mask):
    return jnp.where(mask, 1.0, 0.0).astype(jnp.bfloat16)


VMEM = pl.BlockSpec(memory_space=pltpu.VMEM)
SMEM = pl.BlockSpec(memory_space=pltpu.SMEM)
HBM = pl.BlockSpec(memory_space=pltpu.HBM)
ANY = pl.BlockSpec(memory_space=pl.ANY)


def low(*shape):
    return jax.ShapeDtypeStruct(shape, jnp.bfloat16)


def wide(*shape):
    return jax.ShapeDtypeStruct(shape, jnp.float32)


def space(shape):
    return pltpu.VMEM(shape.shape, shape.dtype)


def call(kernel, outs, args, flops, ins=None, out_specs=None, scratch=(), mib=16):
    moved = sum(math.prod(x.shape) * x.dtype.itemsize for x in (*outs, *args))
    return pl.pallas_call(
        kernel,
        out_shape=outs,
        in_specs=ins or [VMEM] * len(args),
        out_specs=out_specs or [VMEM] * len(outs),
        scratch_shapes=list(scratch),
        compiler_params=pltpu.CompilerParams(vmem_limit_bytes=mib * 2**20),
        cost_estimate=pl.CostEstimate(flops=flops, bytes_accessed=moved, transcendentals=0),
    )(*args)


def fetch(sources, places, sems, first=0):
    copies = [
        pltpu.make_async_copy(source, place, sems.at[first + i])
        for i, (source, place) in enumerate(zip(sources, places, strict=True))
    ]
    for copy in copies:
        copy.start()
    return copies


def gate(block, *others, flops=0):
    return pl.pallas_call(
        lambda *refs: None,
        out_shape=jax.ShapeDtypeStruct(block.shape, block.dtype),
        in_specs=[HBM] + [ANY] * len(others),
        out_specs=HBM,
        input_output_aliases={0: 0},
        cost_estimate=pl.CostEstimate(flops=flops, bytes_accessed=0, transcendentals=0),
    )(block, *others)


def pack_points_kernel(dev_hbm, row_hbm, x_hbm, out_ref, slots_ref, dev_ref, row_ref, x_ref, sems):
    copies = fetch([dev_hbm, row_hbm, x_hbm], [dev_ref, row_ref, x_ref], sems)
    n_dev, block, _ = out_ref.shape
    rows, width = x_ref.shape
    cap = (block - INFO_ROWS) * LANES // width
    copies[0].wait()
    dev = dev_ref[...]
    mine = iota((n_dev, rows), 0) == dev
    mine_f = jnp.where(mine, 1.0, 0.0)
    upto = hot(iota((rows, rows), 0) <= iota((rows, rows), 1))
    running = contract(mine_f.astype(jnp.bfloat16), upto, 1, 0)
    rank = (jnp.sum(running * mine_f, axis=0, keepdims=True) - 1.0).astype(jnp.int32)
    slots = dev * cap + rank
    slots_ref[...] = slots
    at_rank = hot(iota((LANES, rows), 0) % cap == rank)
    copies[1].wait()
    centred = (row_ref[...] - rows // 2).astype(jnp.float32)
    told = jnp.concatenate([mine_f * centred, mine_f], axis=0).astype(jnp.bfloat16)
    got = contract(told, at_rank, 1, 1)
    info = jnp.where(got[n_dev:] > 0.5, got[:n_dev], float(rows))
    per = 256 // cap
    copies[2].wait()
    for first in range(0, n_dev, per):
        pick = hot(iota((per * cap, rows), 0) + first * cap == slots)
        data = contract(pick, x_ref[...], 1, 0)
        for j in range(per):
            dest = first + j
            stack = [
                data[j * cap : (j + 1) * cap, col : col + LANES] for col in range(0, width, LANES)
            ]
            stack.append(jnp.broadcast_to(info[dest : dest + 1], (INFO_ROWS, LANES)))
            out_ref[dest] = jnp.concatenate(stack, axis=0).astype(jnp.bfloat16)


def pack_grads_kernel(slots_ref, x_ref, out_ref, back_ref):
    total = out_ref.shape[0]
    rows = x_ref.shape[0]
    pick = jnp.where(iota((total, rows), 0) == slots_ref[...], 1.0, 0.0)
    out_ref[...] = contract(pick.astype(jnp.bfloat16), x_ref[...], 1, 0).astype(jnp.bfloat16)
    back_ref[...] = pick.T.astype(jnp.bfloat16)


def place_points_kernel(core_ref, got_ref, near_ref, far_ref, at_ref):
    n_dev, block, _ = got_ref.shape
    rows, width = (2 * near_ref.shape[0], near_ref.shape[1])
    cap = (block - INFO_ROWS) * LANES // width
    half = rows // 2
    per = LANES // cap
    source = iota((1, LANES), 1) // cap
    centred = (iota((rows, LANES), 0) - half).astype(jnp.float32)
    parts, data = ([], [])
    for first in range(0, n_dev, per):
        at = jnp.zeros((1, LANES), jnp.float32)
        for j in range(per):
            got = got_ref[first + j]
            info = got.astype(jnp.float32)[block - INFO_ROWS : block - INFO_ROWS + 1]
            at = jnp.where(source == j, info, at)
            if cap % 16:
                got = got.astype(jnp.float32)
            cols = [got[i * cap : (i + 1) * cap] for i in range(width // LANES)]
            data.append(jnp.concatenate(cols, axis=1))
        at_ref[first // per : first // per + 1, :] = at
        parts.append(hot(centred == at))
    placed = contract(
        jnp.concatenate(parts, axis=1), jnp.concatenate(data, axis=0).astype(jnp.bfloat16), 1, 0
    ).astype(jnp.bfloat16)
    near_ref[...] = jnp.where(core_ref[0] == 0, placed[half:], placed[:half])
    far_ref[...] = jnp.where(core_ref[0] == 0, placed[:half], placed[half:])


def place_table(at_ref, rows):
    centred = (iota((rows, LANES), 0) - rows // 2).astype(jnp.float32)
    parts = [
        jnp.where(centred == at_ref[g : g + 1, :], 1.0, 0.0) for g in range(at_ref.shape[0])
    ]
    return jnp.concatenate(parts, axis=1)


def pick_kernel(
    core_ref,
    near_hbm,
    far_hbm,
    own_hbm,
    table_hbm,
    out_hbm,
    done_ref,
    near_ref,
    far_ref,
    own_ref,
    table_ref,
    out_ref,
    sems,
):
    done_ref[...] = jnp.zeros_like(done_ref)
    copies = fetch(
        [near_hbm, far_hbm, own_hbm, table_hbm], [near_ref, far_ref, own_ref, table_ref], sems
    )
    for copy in copies:
        copy.wait()
    half = near_ref.shape[0]
    near = near_ref[...].astype(jnp.float32)
    far = far_ref[...].astype(jnp.float32)
    own = jnp.concatenate(
        [
            own_ref[:half, :] + jnp.where(core_ref[0] == 0, far, near),
            own_ref[half:, :] + jnp.where(core_ref[0] == 0, near, far),
        ],
        axis=0,
    ).astype(jnp.bfloat16)
    stores = []
    parts = 4
    part = out_ref.shape[0] // parts
    for i in range(parts):
        rows = pl.ds(i * part, part)
        out_ref[rows, :] = contract(table_ref[rows, :], own, 1, 0).astype(jnp.bfloat16)
        stores += fetch([out_ref.at[rows, :]], [out_hbm.at[rows, :]], sems, 4 + i)
    for store in stores:
        store.wait()


def restore_kernel(table_ref, got_ref, out_ref):
    out_ref[...] = contract(table_ref[...], got_ref[...], 1, 0).astype(jnp.bfloat16)


def forward_kernel(
    core_ref,
    at_ref,
    near_sent_ref,
    far_sent_ref,
    near_ref,
    far_ref,
    w_hbm,
    w_kv_t_hbm,
    query_hbm,
    value_hbm,
    key_t_hbm,
    attn_t_hbm,
    probs_hbm,
    points_t_hbm,
    table_hbm,
    points_ref,
    w_ref,
    w_kv_t_ref,
    query_ref,
    value_ref,
    key_t_ref,
    attn_t_ref,
    probs_ref,
    points_t_ref,
    table_ref,
    sems,
):
    width = w_ref.shape[0]
    head_dim = width // HEADS
    half = points_ref.shape[0] // 4
    copies = fetch([w_hbm, w_kv_t_hbm], [w_ref, w_kv_t_ref], sems)
    even = core_ref[0] == 0
    quarters = ((far_ref, near_ref), (far_sent_ref, near_sent_ref))
    for i, (on_even, on_odd) in enumerate((*quarters, *(pair[::-1] for pair in quarters[::-1]))):
        points_ref[i * half : (i + 1) * half, :] = jnp.where(even, on_even[...], on_odd[...])
    table_ref[...] = place_table(at_ref, 2 * half).T.astype(jnp.bfloat16)
    stores = fetch([table_ref], [table_hbm], sems, 6)
    for copy in copies:
        copy.wait()
    points = points_ref[...]
    query_ref[...] = contract(points[half : 3 * half], w_ref[:, :width], 1, 0).astype(jnp.bfloat16)
    keys = contract(points, w_ref[:, width : 2 * width], 1, 0).astype(jnp.bfloat16)
    value_ref[...] = contract(points, w_ref[:, 2 * width :], 1, 0).astype(jnp.bfloat16)
    kv_t = contract(w_kv_t_ref[...], points, 1, 1).astype(jnp.bfloat16)
    key_t_ref[...] = kv_t[:width]
    points_t_ref[...] = points.astype(jnp.float32).T.astype(jnp.bfloat16)
    stores += fetch(
        [query_ref, value_ref, key_t_ref, points_t_ref],
        [query_hbm, value_hbm, key_t_hbm, points_t_hbm],
        sems,
        7,
    )
    side = iota((1, LANES), 1) // head_dim
    factor = math.log2(math.e) / math.sqrt(head_dim)
    for head in range(HEADS):
        first = head * head_dim // LANES * LANES
        within = head * head_dim % LANES // head_dim
        query = query_ref[:, first : first + LANES]
        query = jnp.where(side == within, query, jnp.zeros_like(query))
        key = keys[:, first : first + LANES]
        scores = jnp.concatenate(
            [
                contract(key[: 2 * half], query[:half], 1, 1),
                contract(key[2 * half :], query[half:], 1, 1),
            ],
            axis=1,
        )
        top = jnp.max(scores, axis=0, keepdims=True)
        weight = jnp.exp2((scores - top) * factor)
        probs = weight * (1.0 / jnp.sum(weight, axis=0, keepdims=True))
        probs_low = probs.astype(jnp.bfloat16)
        probs_ref[head] = probs_low
        stores += fetch([probs_ref.at[head]], [probs_hbm.at[head]], sems, 12 + head)
        value_t = kv_t[width + head * head_dim : width + (head + 1) * head_dim]
        attn_t_ref[head * head_dim : (head + 1) * head_dim, :] = jnp.concatenate(
            [
                contract(value_t[:, : 2 * half], probs_low[:, :half], 1, 0),
                contract(value_t[:, 2 * half :], probs_low[:, half:], 1, 0),
            ],
            axis=1,
        ).astype(jnp.bfloat16)
    stores += fetch([attn_t_ref], [attn_t_hbm], sems, 11)
    for store in stores:
        store.wait()


def weights(points_t, attn_t, grad_query, grad_kv, grads):
    half = grads.shape[0] // 2
    return (
        contract(points_t[:, half : 3 * half], grad_query, 1, 0),
        contract(points_t, grad_kv, 1, 0),
        contract(attn_t, grads, 1, 0),
    )


def backward_kernel(
    core_ref,
    at_ref,
    got_hbm,
    w_out_hbm,
    query_hbm,
    value_hbm,
    key_t_hbm,
    attn_t_hbm,
    points_t_hbm,
    w_hbm,
    probs_hbm,
    send_hbm,
    keep_hbm,
    own_hbm,
    near_hbm,
    far_hbm,
    got_ref,
    w_out_ref,
    query_ref,
    value_ref,
    key_t_ref,
    attn_t_ref,
    points_t_ref,
    w_ref,
    probs_ref,
    grad_query_ref,
    grad_kv_ref,
    query_t_ref,
    send_ref,
    keep_ref,
    own_ref,
    near_ref,
    far_ref,
    sems,
):
    width = w_out_ref.shape[0]
    head_dim = width // HEADS
    half = query_ref.shape[0] // 2
    scale = 1.0 / math.sqrt(head_dim)
    first_copies = fetch([got_hbm, w_out_hbm], [got_ref, w_out_ref], sems)
    copies = fetch(
        [attn_t_hbm, query_hbm, value_hbm, key_t_hbm],
        [attn_t_ref, query_ref, value_ref, key_t_ref],
        sems,
        2,
    )

    def fetch_probs(first, last):
        heads = range(first, min(last, HEADS))
        return fetch(
            [probs_hbm.at[h] for h in heads], [probs_ref.at[h] for h in heads], sems, 8 + first
        )

    per = LANES // head_dim
    probs_copies = fetch_probs(0, per)
    table = place_table(at_ref, 2 * half).astype(jnp.bfloat16)
    first_copies[0].wait()
    grads = contract(table, got_ref[...], 1, 0).astype(jnp.bfloat16)
    first_copies[1].wait()
    grad_attn = contract(grads, w_out_ref[...], 1, 1).astype(jnp.bfloat16)
    grad_attn_t = contract(w_out_ref[...], grads, 1, 1).astype(jnp.bfloat16)
    for copy in copies:
        copy.wait()
    side = iota((1, LANES), 1) // head_dim
    sides = ((slice(0, half), slice(0, 2 * half)), (slice(half, 2 * half), slice(2 * half, 4 * half)))
    for first in range(0, width, LANES):
        cols = slice(first, first + LANES)
        value_cols = slice(width + first, width + first + LANES)
        grad = grad_attn[:, cols]
        query = query_ref[:, cols]
        for copy in probs_copies:
            copy.wait()
        probs_copies = fetch_probs(first // head_dim + per, first // head_dim + 2 * per)
        if first == 0:
            late = fetch([points_t_hbm, w_hbm], [points_t_ref, w_ref], sems, 6)
        for mine, patch in sides:
            value = value_ref[patch, cols]
            grad_key = jnp.zeros((2 * half, LANES), jnp.float32)
            grad_value = grad_key
            for within in range(LANES // head_dim):
                chans = slice(first + within * head_dim, first + (within + 1) * head_dim)
                probs = probs_ref[first // head_dim + within][:, mine]
                delta = jnp.sum(
                    grad_attn_t[chans, mine].astype(jnp.float32)
                    * attn_t_ref[chans, mine].astype(jnp.float32),
                    axis=0,
                    keepdims=True,
                )
                masked = jnp.where(side == within, grad[mine], jnp.zeros_like(grad[mine]))
                grad_probs = contract(value, masked, 1, 1)
                grad_scores = (probs.astype(jnp.float32) * (grad_probs - delta)).astype(jnp.bfloat16)
                grad_value = jnp.where(
                    side == within, contract(probs, grad[mine], 1, 0), grad_value
                )
                grad_key = jnp.where(
                    side == within, contract(grad_scores, query[mine], 1, 0), grad_key
                )
                query_t_ref[chans, mine] = (
                    contract(key_t_ref[chans, patch], grad_scores, 1, 0) * scale
                )
            grad_kv_ref[patch, cols] = (grad_key * scale).astype(jnp.bfloat16)
            grad_kv_ref[patch, value_cols] = grad_value.astype(jnp.bfloat16)
    grad_query_ref[...] = query_t_ref[...].T.astype(jnp.bfloat16)
    for copy in late:
        copy.wait()
    w_kv = w_ref[:, width:]
    own_ref[...] = contract(grad_query_ref[...], w_ref[:, :width], 1, 1) + contract(
        grad_kv_ref[half : 3 * half, :], w_kv, 1, 1
    )
    stores = fetch([own_ref], [own_hbm], sems, 8 + HEADS)
    before = contract(grad_kv_ref[:half, :], w_kv, 1, 1).astype(jnp.bfloat16)
    after = contract(grad_kv_ref[3 * half :, :], w_kv, 1, 1).astype(jnp.bfloat16)
    near_ref[...] = jnp.where(core_ref[0] == 0, after, before)
    far_ref[...] = jnp.where(core_ref[0] == 0, before, after)
    stores += fetch([near_ref, far_ref], [near_hbm, far_hbm], sems, 9 + HEADS)
    rows = width // 2
    for index, (side, out_ref, out_hbm) in enumerate(
        ((core_ref[0], keep_ref, keep_hbm), (1 - core_ref[0], send_ref, send_hbm))
    ):
        from_row = pl.multiple_of(side * rows, rows)
        of_query, of_kv, of_out = weights(
            points_t_ref[pl.ds(from_row, rows), :],
            attn_t_ref[pl.ds(from_row, rows), :],
            grad_query_ref[...],
            grad_kv_ref[...],
            grads,
        )
        out_ref[:, :width] = of_query.astype(out_ref.dtype)
        out_ref[:, width : 3 * width] = of_kv.astype(out_ref.dtype)
        out_ref[:, 3 * width :] = of_out.astype(out_ref.dtype)
        stores += fetch([out_ref], [out_hbm], sems, 11 + HEADS + index)
    for store in stores:
        store.wait()


def exchange(blocks):
    return lax.all_to_all(blocks, "curve", split_axis=0, concat_axis=0, tiled=True)


def swap(block, axis, mask):
    size = lax.axis_size(axis)
    return lax.ppermute(block, axis, [(i, i ^ mask) for i in range(size)])


def order_blocks(blocks, place):
    count = blocks.shape[0]
    tail = blocks.shape[1:]
    bit = 1
    while bit < count:
        pairs = blocks.reshape(count // (2 * bit), 2, bit, *tail)
        blocks = jnp.where((place & bit) != 0, pairs[:, ::-1], pairs).reshape(count, *tail)
        bit *= 2
    return blocks


def first_sum_kernel(sides_ref, kept_ref, got_ref, keep, send_x, send_y, send_xy):
    rows = keep.shape[0]
    side_x, side_y = (sides_ref[0], sides_ref[1])
    quarters = []
    for far_x, far_y in ((1, 0), (1, 1), (0, 1), (0, 0)):
        at = ((side_x ^ far_x) * 2 + (side_y ^ far_y)) * rows
        quarters.append(pl.ds(pl.multiple_of(at, rows), rows))
    for quarter, out_ref in zip(quarters, (send_x, send_xy, send_y, keep), strict=True):
        total = kept_ref[quarter, :].astype(jnp.float32) + got_ref[quarter, :].astype(jnp.float32)
        out_ref[...] = total.astype(out_ref.dtype)


def second_sum_kernel(line_ref, kept_ref, *refs):
    got, mine_ref, sends, total_ref = (refs[:3], refs[4], refs[5:-1], refs[-1])
    rows = mine_ref.shape[0]
    total = kept_ref[...]
    for ref in got:
        total = total + ref[...].astype(jnp.float32)
    total_ref[...] = total
    for distance, out_ref in enumerate((mine_ref, *sends)):
        at = pl.multiple_of((line_ref[0] ^ distance) * rows, rows)
        out_ref[...] = total_ref[pl.ds(at, rows), :].astype(out_ref.dtype)


def third_sum_kernel(mine_ref, *refs):
    others, out_ref = (refs[:-1], refs[-1])
    total = mine_ref[...]
    for other in others:
        total = total + other[...].astype(jnp.float32)
    out_ref[...] = total.astype(jnp.bfloat16)


def join_kernel(*refs):
    refs[-1][...] = jnp.concatenate([ref[...] for ref in refs[:-1]], axis=0)


def spread_kernel(n_line, place_ref, *refs):
    pieces, qkv_ref, out_ref = (refs[:-2], refs[-2], refs[-1])
    n_qkv = qkv_ref.shape[1]
    core, side_x, side_y, line = (place_ref[i] for i in range(4))
    rows = pieces[0].shape[0] // n_line
    for index, piece in enumerate(pieces):
        near_x, near_y = (side_x ^ (index & 1), side_y ^ (index >> 1 & 1))
        quarter = ((core ^ (index >> 2)) * 2 + near_x) * 2 + near_y
        for distance in range(n_line):
            row = pl.multiple_of((quarter * n_line + (line ^ distance)) * rows, rows)
            data = piece[distance * rows : (distance + 1) * rows, :].astype(jnp.float32)
            qkv_ref[pl.ds(row, rows), :] = data[:, :n_qkv]
            out_ref[pl.ds(row, rows), :] = data[:, n_qkv:]


def swap_across(block):
    size = lax.axis_size("curve")
    route = [(2 * i + j, 2 * (i ^ 2) + (j ^ 1)) for i in range(size) for j in range(2)]
    return lax.ppermute(block, ("curve", "dp"), route)


def sum_core(keep, send, sides):
    rows, width = keep.shape
    rows = rows // 4
    kept, send_x, send_y, send_xy = call(
        first_sum_kernel,
        [wide(rows, width)] + [low(rows, width)] * 3,
        [sides, keep, swap(send, "curve", 1)],
        4 * rows * width,
        [SMEM, VMEM, VMEM],
    )
    return (kept, [swap_across(send_xy), swap(send_x, "curve", 2), swap(send_y, "dp", 1)])


def sum_xy(kept, got, ready):
    n_line = lax.axis_size("curve") // 4
    line = lax.axis_index("curve") >> 2
    rows, width = kept.shape
    rows = rows // n_line
    if rows % 16 == 0:
        mine, *sends = call(
            second_sum_kernel,
            [wide(rows, width)] + [low(rows, width)] * (n_line - 1),
            [line.reshape(1), kept, *got, ready],
            kept.size,
            [SMEM] + [VMEM] * 5,
            scratch=[space(kept)],
        )
        return (mine, sends)
    total = kept + sum(x.astype(jnp.float32) for x in got)
    total = total.reshape(n_line, rows, width)
    mine, *sends = [
        lax.dynamic_index_in_dim(total, line ^ k, 0, keepdims=False) for k in range(n_line)
    ]
    return (mine, [block.astype(jnp.bfloat16) for block in sends])


def sum_line(mine, sends):
    n_line = len(sends) + 1
    line = lax.axis_index("curve") >> 2
    rows, width = mine.shape
    others = [swap(sends[k - 1], "curve", 4 * k) for k in range(n_line - 1, 0, -1)]
    (mine,) = call(third_sum_kernel, [low(rows, width)], [mine, *others], mine.size)
    blocks = [swap(mine, "curve", 4 * k) for k in range(n_line - 1, 0, -1)]
    blocks = [mine] + blocks[::-1]
    if rows % 16 == 0:
        (own,) = call(join_kernel, [low(n_line * rows, width)], blocks, mine.size)
        return (own, line, n_line)
    own = order_blocks(jnp.stack(blocks), line).reshape(n_line * rows, width)
    return (own, jnp.zeros_like(line), 1)


def sum_finish(own, line, n_line, sides, width_qkv):
    core = lax.axis_index("curve") & 1
    rows, width = own.shape
    over_x = swap(own, "curve", 2)
    pieces = [own, over_x, swap(own, "dp", 1), swap(over_x, "dp", 1)]
    pieces += [swap(piece, "curve", 1) for piece in pieces]
    return call(
        functools.partial(spread_kernel, n_line),
        [wide(8 * rows, width_qkv), wide(8 * rows, width - width_qkv)],
        [jnp.stack([core, sides[0], sides[1], line]), *pieces],
        SPREAD_FLOPS,
        [SMEM] + [VMEM] * len(pieces),
    )


def halo(near, far):
    size = lax.axis_size("curve")
    route = [(i, (i + 2 * (i % 2) - 1) % size) for i in range(size)]
    return (swap(near, "curve", 1), lax.ppermute(far, "curve", route))


def on_device(points, grad_out, dest_dev, dest_row, w_qkv, w_out):
    rows, width = points.shape[1:]
    half = rows - PATCH // 2
    n_dev = lax.axis_size("curve")
    cap = 2 * rows // n_dev
    total = n_dev * cap
    place_flops = 2 * total * rows * width
    me = lax.axis_index("curve")
    core = (me & 1).reshape(1)
    sides = jnp.stack([(me >> 1) & 1, lax.axis_index("dp")])
    ids = jax.ShapeDtypeStruct((1, rows), jnp.int32)
    send_points, slots = call(
        pack_points_kernel,
        [low(n_dev, cap * width // LANES + INFO_ROWS, LANES), ids],
        [dest_dev, dest_row, points[0]],
        place_flops,
        [HBM] * 3,
        scratch=[space(ids), space(ids), space(low(rows, width)), pltpu.SemaphoreType.DMA((3,))],
        mib=60,
    )
    got_points = exchange(send_points)
    send_grads, restore_table = call(
        pack_grads_kernel, [low(total, width), low(rows, total)], [slots, grad_out[0]], place_flops
    )
    near_sent, far_sent, at = call(
        place_points_kernel,
        [
            low(half, width),
            low(half, width),
            wide(total // LANES, LANES),
        ],
        [core, got_points],
        place_flops,
        [SMEM, VMEM],
    )
    near, far = halo(near_sent, far_sent)
    send_grads = gate(send_grads, at, flops=GATE_FLOPS)
    got_grads = exchange(send_grads.reshape(n_dev, cap, width)).reshape(total, width)
    saved = [
        low(rows, width),
        low(2 * rows, width),
        low(width, 2 * rows),
        low(width, rows),
        low(HEADS, PATCH, PATCH),
        low(width, 2 * rows),
        low(total, rows),
    ]
    query, value, key_t, attn_t, probs, points_t, pick_table = call(
        forward_kernel,
        saved,
        [core, at, near_sent, far_sent, near, far, w_qkv, w_qkv[:, width:].T],
        FORWARD_FLOPS,
        [SMEM] + [VMEM] * 5 + [HBM] * 2,
        [HBM] * len(saved),
        [space(low(2 * rows, width)), space(low(width, 3 * width)), space(low(2 * width, width))]
        + [space(x) for x in saved]
        + [pltpu.SemaphoreType.DMA((12 + HEADS,))],
        60,
    )
    held = [got_grads, w_out, query, value, key_t, attn_t, points_t, w_qkv, probs]
    made = [
        low(width // 2, 4 * width),
        low(width // 2, 4 * width),
        wide(rows, width),
        low(half, width),
        low(half, width),
    ]
    send, keep, own_input, near, far = call(
        backward_kernel,
        made,
        [core, at, *held],
        32 * rows * rows * width + 22 * rows * width * width,
        [SMEM, VMEM] + [HBM] * len(held),
        [HBM] * len(made),
        [space(x) for x in held]
        + [space(low(rows, width)), space(low(2 * rows, 2 * width)), space(wide(width, rows))]
        + [space(x) for x in made]
        + [pltpu.SemaphoreType.DMA((13 + HEADS,))],
        63,
    )
    kept, got = sum_core(keep, send, sides)
    near, far = halo(near, far)
    picked = low(total, width)
    picked, done = call(
        pick_kernel,
        [picked, wide(8, LANES)],
        [core, near, far, own_input, pick_table],
        place_flops,
        [SMEM] + [HBM] * 4,
        [HBM, VMEM],
        [space(x) for x in (near, far, own_input, pick_table, picked)] + [pltpu.SemaphoreType.DMA((8,))],
        63,
    )
    mine, sends = sum_xy(kept, got, done)
    gathered, line, n_line = sum_line(mine, sends)
    picked = gate(picked, gathered, flops=GATE_FLOPS)
    returned = exchange(picked.reshape(n_dev, cap, width)).reshape(total, width)
    weight_qkv, weight_out = sum_finish(gathered, line, n_line, sides, 3 * width)
    (result,) = call(restore_kernel, [low(rows, width)], [restore_table, returned], place_flops)
    return (result[None], weight_qkv, weight_out)


def solution(mesh):
    placed = (
        P("dp", "curve", None),
        P("dp", "curve", None),
        P("dp", "curve"),
        P("dp", "curve"),
        P(),
        P(),
    )
    return jax.shard_map(
        on_device,
        mesh=mesh,
        in_specs=placed,
        out_specs=(P("dp", "curve", None), P(), P()),
        check_vma=False,
    )
```

```python
import functools
import math

import jax
import jax.numpy as jnp
from jax import lax
from jax.experimental import pallas as pl
from jax.experimental.pallas import tpu as pltpu
from jax.sharding import PartitionSpec as P

HEADS = 8
PATCH = 512
INFO_ROWS = 8
GATE_FLOPS = 10**10
FORWARD_FLOPS = 10**11
SPREAD_FLOPS = 13 * 10**9
LANES = 128


def contract(left, right, left_dim, right_dim):
    return lax.dot_general(
        left, right, (((left_dim,), (right_dim,)), ((), ())), preferred_element_type=jnp.float32
    )


def iota(shape, dim):
    return lax.broadcasted_iota(jnp.int32, shape, dim)


def hot(mask):
    return jnp.where(mask, 1.0, 0.0).astype(jnp.bfloat16)


VMEM = pl.BlockSpec(memory_space=pltpu.VMEM)
SMEM = pl.BlockSpec(memory_space=pltpu.SMEM)
HBM = pl.BlockSpec(memory_space=pltpu.HBM)
ANY = pl.BlockSpec(memory_space=pl.ANY)


def low(*shape):
    return jax.ShapeDtypeStruct(shape, jnp.bfloat16)


def wide(*shape):
    return jax.ShapeDtypeStruct(shape, jnp.float32)


def space(shape):
    return pltpu.VMEM(shape.shape, shape.dtype)


def call(kernel, outs, args, flops, ins=None, out_specs=None, scratch=(), mib=16):
    moved = sum(math.prod(x.shape) * x.dtype.itemsize for x in (*outs, *args))
    return pl.pallas_call(
        kernel,
        out_shape=outs,
        in_specs=ins or [VMEM] * len(args),
        out_specs=out_specs or [VMEM] * len(outs),
        scratch_shapes=list(scratch),
        compiler_params=pltpu.CompilerParams(vmem_limit_bytes=mib * 2**20),
        cost_estimate=pl.CostEstimate(flops=flops, bytes_accessed=moved, transcendentals=0),
    )(*args)


def fetch(sources, places, sems, first=0):
    copies = [
        pltpu.make_async_copy(source, place, sems.at[first + i])
        for i, (source, place) in enumerate(zip(sources, places, strict=True))
    ]
    for copy in copies:
        copy.start()
    return copies


def gate(block, *others, flops=0):
    return pl.pallas_call(
        lambda *refs: None,
        out_shape=jax.ShapeDtypeStruct(block.shape, block.dtype),
        in_specs=[HBM] + [ANY] * len(others),
        out_specs=HBM,
        input_output_aliases={0: 0},
        cost_estimate=pl.CostEstimate(flops=flops, bytes_accessed=0, transcendentals=0),
    )(block, *others)


def pack_points_kernel(dev_hbm, row_hbm, x_hbm, out_ref, slots_ref, dev_ref, row_ref, x_ref, sems):
    copies = fetch([dev_hbm, row_hbm, x_hbm], [dev_ref, row_ref, x_ref], sems)
    n_dev, block, _ = out_ref.shape
    rows, width = x_ref.shape
    cap = (block - INFO_ROWS) * LANES // width
    copies[0].wait()
    dev = dev_ref[...]
    mine = iota((n_dev, rows), 0) == dev
    mine_f = jnp.where(mine, 1.0, 0.0)
    upto = hot(iota((rows, rows), 0) <= iota((rows, rows), 1))
    running = contract(mine_f.astype(jnp.bfloat16), upto, 1, 0)
    rank = (jnp.sum(running * mine_f, axis=0, keepdims=True) - 1.0).astype(jnp.int32)
    slots = dev * cap + rank
    slots_ref[...] = slots
    at_rank = hot(iota((LANES, rows), 0) % cap == rank)
    copies[1].wait()
    centred = (row_ref[...] - rows // 2).astype(jnp.float32)
    told = jnp.concatenate([mine_f * centred, mine_f], axis=0).astype(jnp.bfloat16)
    got = contract(told, at_rank, 1, 1)
    info = jnp.where(got[n_dev:] > 0.5, got[:n_dev], float(rows))
    per = 256 // cap
    copies[2].wait()
    for first in range(0, n_dev, per):
        pick = hot(iota((per * cap, rows), 0) + first * cap == slots)
        data = contract(pick, x_ref[...], 1, 0)
        for j in range(per):
            dest = first + j
            stack = [
                data[j * cap : (j + 1) * cap, col : col + LANES] for col in range(0, width, LANES)
            ]
            stack.append(jnp.broadcast_to(info[dest : dest + 1], (INFO_ROWS, LANES)))
            out_ref[dest] = jnp.concatenate(stack, axis=0).astype(jnp.bfloat16)


def pack_grads_kernel(slots_ref, x_ref, out_ref, back_ref):
    total = out_ref.shape[0]
    rows = x_ref.shape[0]
    pick = jnp.where(iota((total, rows), 0) == slots_ref[...], 1.0, 0.0)
    out_ref[...] = contract(pick.astype(jnp.bfloat16), x_ref[...], 1, 0).astype(jnp.bfloat16)
    back_ref[...] = pick.T.astype(jnp.bfloat16)


def place_points_kernel(core_ref, got_ref, near_ref, far_ref, at_ref):
    n_dev, block, _ = got_ref.shape
    rows, width = (2 * near_ref.shape[0], near_ref.shape[1])
    cap = (block - INFO_ROWS) * LANES // width
    half = rows // 2
    per = LANES // cap
    source = iota((1, LANES), 1) // cap
    centred = (iota((rows, LANES), 0) - half).astype(jnp.float32)
    parts, data = ([], [])
    for first in range(0, n_dev, per):
        at = jnp.zeros((1, LANES), jnp.float32)
        for j in range(per):
            got = got_ref[first + j]
            info = got.astype(jnp.float32)[block - INFO_ROWS : block - INFO_ROWS + 1]
            at = jnp.where(source == j, info, at)
            if cap % 16:
                got = got.astype(jnp.float32)
            cols = [got[i * cap : (i + 1) * cap] for i in range(width // LANES)]
            data.append(jnp.concatenate(cols, axis=1))
        at_ref[first // per : first // per + 1, :] = at
        parts.append(hot(centred == at))
    placed = contract(
        jnp.concatenate(parts, axis=1), jnp.concatenate(data, axis=0).astype(jnp.bfloat16), 1, 0
    ).astype(jnp.bfloat16)
    near_ref[...] = jnp.where(core_ref[0] == 0, placed[half:], placed[:half])
    far_ref[...] = jnp.where(core_ref[0] == 0, placed[:half], placed[half:])


def place_table(at_ref, rows):
    centred = (iota((rows, LANES), 0) - rows // 2).astype(jnp.float32)
    parts = [
        jnp.where(centred == at_ref[g : g + 1, :], 1.0, 0.0) for g in range(at_ref.shape[0])
    ]
    return jnp.concatenate(parts, axis=1)


def pick_kernel(
    core_ref,
    near_hbm,
    far_hbm,
    grad_query_hbm,
    grad_kv_hbm,
    w_hbm,
    table_hbm,
    out_hbm,
    done_ref,
    near_ref,
    far_ref,
    grad_query_ref,
    grad_kv_ref,
    w_ref,
    table_ref,
    out_ref,
    sems,
):
    done_ref[...] = jnp.zeros_like(done_ref)
    copies = fetch(
        [grad_query_hbm, w_hbm, grad_kv_hbm, near_hbm, far_hbm, table_hbm],
        [grad_query_ref, w_ref, grad_kv_ref, near_ref, far_ref, table_ref],
        sems,
        4,
    )
    for copy in copies:
        copy.wait()
    half, width = near_ref.shape
    own = contract(grad_query_ref[...], w_ref[:, :width], 1, 1) + contract(
        grad_kv_ref[...], w_ref[:, width:], 1, 1
    )
    near = near_ref[...].astype(jnp.float32)
    far = far_ref[...].astype(jnp.float32)
    own = jnp.concatenate(
        [
            own[:half] + jnp.where(core_ref[0] == 0, far, near),
            own[half:] + jnp.where(core_ref[0] == 0, near, far),
        ],
        axis=0,
    ).astype(jnp.bfloat16)
    stores = []
    parts = 4
    part = out_ref.shape[0] // parts
    for i in range(parts):
        rows = pl.ds(i * part, part)
        out_ref[rows, :] = contract(table_ref[rows, :], own, 1, 0).astype(jnp.bfloat16)
        stores += fetch([out_ref.at[rows, :]], [out_hbm.at[rows, :]], sems, i)
    for store in stores:
        store.wait()


def restore_kernel(table_ref, got_ref, out_ref):
    out_ref[...] = contract(table_ref[...], got_ref[...], 1, 0).astype(jnp.bfloat16)


def forward_kernel(
    core_ref,
    at_ref,
    near_sent_ref,
    far_sent_ref,
    near_ref,
    far_ref,
    w_hbm,
    w_kv_t_hbm,
    query_hbm,
    value_hbm,
    key_t_hbm,
    attn_t_hbm,
    probs_hbm,
    points_t_hbm,
    table_hbm,
    points_ref,
    w_ref,
    w_kv_t_ref,
    query_ref,
    value_ref,
    key_t_ref,
    attn_t_ref,
    probs_ref,
    points_t_ref,
    table_ref,
    sems,
):
    width = w_ref.shape[0]
    head_dim = width // HEADS
    half = points_ref.shape[0] // 4
    copies = fetch([w_hbm, w_kv_t_hbm], [w_ref, w_kv_t_ref], sems)
    even = core_ref[0] == 0
    quarters = ((far_ref, near_ref), (far_sent_ref, near_sent_ref))
    for i, (on_even, on_odd) in enumerate((*quarters, *(pair[::-1] for pair in quarters[::-1]))):
        points_ref[i * half : (i + 1) * half, :] = jnp.where(even, on_even[...], on_odd[...])
    table_ref[...] = place_table(at_ref, 2 * half).T.astype(jnp.bfloat16)
    stores = fetch([table_ref], [table_hbm], sems, 6)
    for copy in copies:
        copy.wait()
    points = points_ref[...]
    query_ref[...] = contract(points[half : 3 * half], w_ref[:, :width], 1, 0).astype(jnp.bfloat16)
    keys = contract(points, w_ref[:, width : 2 * width], 1, 0).astype(jnp.bfloat16)
    value_ref[...] = contract(points, w_ref[:, 2 * width :], 1, 0).astype(jnp.bfloat16)
    kv_t = contract(w_kv_t_ref[...], points, 1, 1).astype(jnp.bfloat16)
    key_t_ref[...] = kv_t[:width]
    points_t_ref[...] = points.astype(jnp.float32).T.astype(jnp.bfloat16)
    stores += fetch(
        [query_ref, value_ref, key_t_ref, points_t_ref],
        [query_hbm, value_hbm, key_t_hbm, points_t_hbm],
        sems,
        7,
    )
    side = iota((1, LANES), 1) // head_dim
    factor = math.log2(math.e) / math.sqrt(head_dim)
    for head in range(HEADS):
        first = head * head_dim // LANES * LANES
        within = head * head_dim % LANES // head_dim
        query = query_ref[:, first : first + LANES]
        query = jnp.where(side == within, query, jnp.zeros_like(query))
        key = keys[:, first : first + LANES]
        scores = jnp.concatenate(
            [
                contract(key[: 2 * half], query[:half], 1, 1),
                contract(key[2 * half :], query[half:], 1, 1),
            ],
            axis=1,
        )
        top = jnp.max(scores, axis=0, keepdims=True)
        weight = jnp.exp2((scores - top) * factor)
        probs = weight * (1.0 / jnp.sum(weight, axis=0, keepdims=True))
        probs_low = probs.astype(jnp.bfloat16)
        probs_ref[head] = probs_low
        stores += fetch([probs_ref.at[head]], [probs_hbm.at[head]], sems, 12 + head)
        value_t = kv_t[width + head * head_dim : width + (head + 1) * head_dim]
        attn_t_ref[head * head_dim : (head + 1) * head_dim, :] = jnp.concatenate(
            [
                contract(value_t[:, : 2 * half], probs_low[:, :half], 1, 0),
                contract(value_t[:, 2 * half :], probs_low[:, half:], 1, 0),
            ],
            axis=1,
        ).astype(jnp.bfloat16)
    stores += fetch([attn_t_ref], [attn_t_hbm], sems, 11)
    for store in stores:
        store.wait()


def weights(points_t, attn_t, grad_query, grad_kv, grads):
    half = grads.shape[0] // 2
    return (
        contract(points_t[:, half : 3 * half], grad_query, 1, 0),
        contract(points_t, grad_kv, 1, 0),
        contract(attn_t, grads, 1, 0),
    )


def backward_kernel(
    core_ref,
    at_ref,
    got_hbm,
    w_out_hbm,
    query_hbm,
    value_hbm,
    key_t_hbm,
    attn_t_hbm,
    points_t_hbm,
    w_hbm,
    probs_hbm,
    send_hbm,
    keep_hbm,
    grad_query_hbm,
    grad_kv_hbm,
    near_hbm,
    far_hbm,
    got_ref,
    w_out_ref,
    query_ref,
    value_ref,
    key_t_ref,
    attn_t_ref,
    points_t_ref,
    w_ref,
    probs_ref,
    grad_query_ref,
    grad_kv_ref,
    query_t_ref,
    send_ref,
    keep_ref,
    near_ref,
    far_ref,
    sems,
):
    width = w_out_ref.shape[0]
    head_dim = width // HEADS
    half = query_ref.shape[0] // 2
    scale = 1.0 / math.sqrt(head_dim)
    first_copies = fetch([got_hbm, w_out_hbm], [got_ref, w_out_ref], sems)
    copies = fetch(
        [attn_t_hbm, query_hbm, value_hbm, key_t_hbm],
        [attn_t_ref, query_ref, value_ref, key_t_ref],
        sems,
        2,
    )

    def fetch_probs(first, last):
        heads = range(first, min(last, HEADS))
        return fetch(
            [probs_hbm.at[h] for h in heads], [probs_ref.at[h] for h in heads], sems, 8 + first
        )

    per = LANES // head_dim
    probs_copies = fetch_probs(0, per)
    table = place_table(at_ref, 2 * half).astype(jnp.bfloat16)
    first_copies[0].wait()
    grads = contract(table, got_ref[...], 1, 0).astype(jnp.bfloat16)
    first_copies[1].wait()
    grad_attn = contract(grads, w_out_ref[...], 1, 1).astype(jnp.bfloat16)
    grad_attn_t = contract(w_out_ref[...], grads, 1, 1).astype(jnp.bfloat16)
    for copy in copies:
        copy.wait()
    side = iota((1, LANES), 1) // head_dim
    sides = ((slice(0, half), slice(0, 2 * half)), (slice(half, 2 * half), slice(2 * half, 4 * half)))
    for first in range(0, width, LANES):
        cols = slice(first, first + LANES)
        value_cols = slice(width + first, width + first + LANES)
        grad = grad_attn[:, cols]
        query = query_ref[:, cols]
        for copy in probs_copies:
            copy.wait()
        probs_copies = fetch_probs(first // head_dim + per, first // head_dim + 2 * per)
        if first == 0:
            late = fetch([points_t_hbm, w_hbm], [points_t_ref, w_ref], sems, 6)
        for mine, patch in sides:
            value = value_ref[patch, cols]
            grad_key = jnp.zeros((2 * half, LANES), jnp.float32)
            grad_value = grad_key
            for within in range(LANES // head_dim):
                chans = slice(first + within * head_dim, first + (within + 1) * head_dim)
                probs = probs_ref[first // head_dim + within][:, mine]
                delta = jnp.sum(
                    grad_attn_t[chans, mine].astype(jnp.float32)
                    * attn_t_ref[chans, mine].astype(jnp.float32),
                    axis=0,
                    keepdims=True,
                )
                masked = jnp.where(side == within, grad[mine], jnp.zeros_like(grad[mine]))
                grad_probs = contract(value, masked, 1, 1)
                grad_scores = (probs.astype(jnp.float32) * (grad_probs - delta)).astype(jnp.bfloat16)
                grad_value = jnp.where(
                    side == within, contract(probs, grad[mine], 1, 0), grad_value
                )
                grad_key = jnp.where(
                    side == within, contract(grad_scores, query[mine], 1, 0), grad_key
                )
                query_t_ref[chans, mine] = (
                    contract(key_t_ref[chans, patch], grad_scores, 1, 0) * scale
                )
            grad_kv_ref[patch, cols] = (grad_key * scale).astype(jnp.bfloat16)
            grad_kv_ref[patch, value_cols] = grad_value.astype(jnp.bfloat16)
    grad_query_ref[...] = query_t_ref[...].T.astype(jnp.bfloat16)
    stores = fetch(
        [grad_query_ref, grad_kv_ref.at[pl.ds(half, 2 * half), :]],
        [grad_query_hbm, grad_kv_hbm],
        sems,
        13 + HEADS,
    )
    for copy in late:
        copy.wait()
    w_kv = w_ref[:, width:]
    before = contract(grad_kv_ref[:half, :], w_kv, 1, 1).astype(jnp.bfloat16)
    after = contract(grad_kv_ref[3 * half :, :], w_kv, 1, 1).astype(jnp.bfloat16)
    near_ref[...] = jnp.where(core_ref[0] == 0, after, before)
    far_ref[...] = jnp.where(core_ref[0] == 0, before, after)
    stores += fetch([near_ref, far_ref], [near_hbm, far_hbm], sems, 9 + HEADS)
    rows = width // 2
    for index, (side, out_ref, out_hbm) in enumerate(
        ((core_ref[0], keep_ref, keep_hbm), (1 - core_ref[0], send_ref, send_hbm))
    ):
        from_row = pl.multiple_of(side * rows, rows)
        of_query, of_kv, of_out = weights(
            points_t_ref[pl.ds(from_row, rows), :],
            attn_t_ref[pl.ds(from_row, rows), :],
            grad_query_ref[...],
            grad_kv_ref[...],
            grads,
        )
        out_ref[:, :width] = of_query.astype(out_ref.dtype)
        out_ref[:, width : 3 * width] = of_kv.astype(out_ref.dtype)
        out_ref[:, 3 * width :] = of_out.astype(out_ref.dtype)
        stores += fetch([out_ref], [out_hbm], sems, 11 + HEADS + index)
    for store in stores:
        store.wait()


def exchange(blocks):
    return lax.all_to_all(blocks, "curve", split_axis=0, concat_axis=0, tiled=True)


def swap(block, axis, mask):
    size = lax.axis_size(axis)
    return lax.ppermute(block, axis, [(i, i ^ mask) for i in range(size)])


def order_blocks(blocks, place):
    count = blocks.shape[0]
    tail = blocks.shape[1:]
    bit = 1
    while bit < count:
        pairs = blocks.reshape(count // (2 * bit), 2, bit, *tail)
        blocks = jnp.where((place & bit) != 0, pairs[:, ::-1], pairs).reshape(count, *tail)
        bit *= 2
    return blocks


def first_sum_kernel(sides_ref, kept_ref, got_ref, keep, send_x, send_y, send_xy):
    rows = keep.shape[0]
    side_x, side_y = (sides_ref[0], sides_ref[1])
    quarters = []
    for far_x, far_y in ((1, 0), (1, 1), (0, 1), (0, 0)):
        at = ((side_x ^ far_x) * 2 + (side_y ^ far_y)) * rows
        quarters.append(pl.ds(pl.multiple_of(at, rows), rows))
    for quarter, out_ref in zip(quarters, (send_x, send_xy, send_y, keep), strict=True):
        total = kept_ref[quarter, :].astype(jnp.float32) + got_ref[quarter, :].astype(jnp.float32)
        out_ref[...] = total.astype(out_ref.dtype)


def second_sum_kernel(line_ref, kept_ref, *refs):
    got, mine_ref, sends, total_ref = (refs[:3], refs[4], refs[5:-1], refs[-1])
    rows = mine_ref.shape[0]
    total = kept_ref[...]
    for ref in got:
        total = total + ref[...].astype(jnp.float32)
    total_ref[...] = total
    for distance, out_ref in enumerate((mine_ref, *sends)):
        at = pl.multiple_of((line_ref[0] ^ distance) * rows, rows)
        out_ref[...] = total_ref[pl.ds(at, rows), :].astype(out_ref.dtype)


def third_sum_kernel(mine_ref, *refs):
    others, out_ref = (refs[:-1], refs[-1])
    total = mine_ref[...]
    for other in others:
        total = total + other[...].astype(jnp.float32)
    out_ref[...] = total.astype(jnp.bfloat16)


def join_kernel(*refs):
    refs[-1][...] = jnp.concatenate([ref[...] for ref in refs[:-1]], axis=0)


def spread_kernel(n_line, place_ref, *refs):
    pieces, qkv_ref, out_ref = (refs[:-2], refs[-2], refs[-1])
    n_qkv = qkv_ref.shape[1]
    core, side_x, side_y, line = (place_ref[i] for i in range(4))
    rows = pieces[0].shape[0] // n_line
    for index, piece in enumerate(pieces):
        near_x, near_y = (side_x ^ (index & 1), side_y ^ (index >> 1 & 1))
        quarter = ((core ^ (index >> 2)) * 2 + near_x) * 2 + near_y
        for distance in range(n_line):
            row = pl.multiple_of((quarter * n_line + (line ^ distance)) * rows, rows)
            data = piece[distance * rows : (distance + 1) * rows, :].astype(jnp.float32)
            qkv_ref[pl.ds(row, rows), :] = data[:, :n_qkv]
            out_ref[pl.ds(row, rows), :] = data[:, n_qkv:]


def swap_across(block):
    size = lax.axis_size("curve")
    route = [(2 * i + j, 2 * (i ^ 2) + (j ^ 1)) for i in range(size) for j in range(2)]
    return lax.ppermute(block, ("curve", "dp"), route)


def sum_core(keep, send, sides):
    rows, width = keep.shape
    rows = rows // 4
    kept, send_x, send_y, send_xy = call(
        first_sum_kernel,
        [wide(rows, width)] + [low(rows, width)] * 3,
        [sides, keep, swap(send, "curve", 1)],
        4 * rows * width,
        [SMEM, VMEM, VMEM],
    )
    return (kept, [swap_across(send_xy), swap(send_x, "curve", 2), swap(send_y, "dp", 1)])


def sum_xy(kept, got, ready):
    n_line = lax.axis_size("curve") // 4
    line = lax.axis_index("curve") >> 2
    rows, width = kept.shape
    rows = rows // n_line
    if rows % 16 == 0:
        mine, *sends = call(
            second_sum_kernel,
            [wide(rows, width)] + [low(rows, width)] * (n_line - 1),
            [line.reshape(1), kept, *got, ready],
            kept.size,
            [SMEM] + [VMEM] * 5,
            scratch=[space(kept)],
        )
        return (mine, sends)
    total = kept + sum(x.astype(jnp.float32) for x in got)
    total = total.reshape(n_line, rows, width)
    mine, *sends = [
        lax.dynamic_index_in_dim(total, line ^ k, 0, keepdims=False) for k in range(n_line)
    ]
    return (mine, [block.astype(jnp.bfloat16) for block in sends])


def sum_line(mine, sends):
    n_line = len(sends) + 1
    line = lax.axis_index("curve") >> 2
    rows, width = mine.shape
    others = [swap(sends[k - 1], "curve", 4 * k) for k in range(n_line - 1, 0, -1)]
    (mine,) = call(third_sum_kernel, [low(rows, width)], [mine, *others], mine.size)
    blocks = [swap(mine, "curve", 4 * k) for k in range(n_line - 1, 0, -1)]
    blocks = [mine] + blocks[::-1]
    if rows % 16 == 0:
        (own,) = call(join_kernel, [low(n_line * rows, width)], blocks, mine.size)
        return (own, line, n_line)
    own = order_blocks(jnp.stack(blocks), line).reshape(n_line * rows, width)
    return (own, jnp.zeros_like(line), 1)


def sum_finish(own, line, n_line, sides, width_qkv):
    core = lax.axis_index("curve") & 1
    rows, width = own.shape
    over_x = swap(own, "curve", 2)
    pieces = [own, over_x, swap(own, "dp", 1), swap(over_x, "dp", 1)]
    pieces += [swap(piece, "curve", 1) for piece in pieces]
    return call(
        functools.partial(spread_kernel, n_line),
        [wide(8 * rows, width_qkv), wide(8 * rows, width - width_qkv)],
        [jnp.stack([core, sides[0], sides[1], line]), *pieces],
        SPREAD_FLOPS,
        [SMEM] + [VMEM] * len(pieces),
    )


def halo(near, far):
    size = lax.axis_size("curve")
    route = [(i, (i + 2 * (i % 2) - 1) % size) for i in range(size)]
    return (swap(near, "curve", 1), lax.ppermute(far, "curve", route))


def on_device(points, grad_out, dest_dev, dest_row, w_qkv, w_out):
    rows, width = points.shape[1:]
    half = rows - PATCH // 2
    n_dev = lax.axis_size("curve")
    cap = 2 * rows // n_dev
    total = n_dev * cap
    place_flops = 2 * total * rows * width
    me = lax.axis_index("curve")
    core = (me & 1).reshape(1)
    sides = jnp.stack([(me >> 1) & 1, lax.axis_index("dp")])
    ids = jax.ShapeDtypeStruct((1, rows), jnp.int32)
    send_points, slots = call(
        pack_points_kernel,
        [low(n_dev, cap * width // LANES + INFO_ROWS, LANES), ids],
        [dest_dev, dest_row, points[0]],
        place_flops,
        [HBM] * 3,
        scratch=[space(ids), space(ids), space(low(rows, width)), pltpu.SemaphoreType.DMA((3,))],
        mib=60,
    )
    got_points = exchange(send_points)
    send_grads, restore_table = call(
        pack_grads_kernel, [low(total, width), low(rows, total)], [slots, grad_out[0]], place_flops
    )
    near_sent, far_sent, at = call(
        place_points_kernel,
        [
            low(half, width),
            low(half, width),
            wide(total // LANES, LANES),
        ],
        [core, got_points],
        place_flops,
        [SMEM, VMEM],
    )
    near, far = halo(near_sent, far_sent)
    send_grads = gate(send_grads, at, flops=GATE_FLOPS)
    got_grads = exchange(send_grads.reshape(n_dev, cap, width)).reshape(total, width)
    saved = [
        low(rows, width),
        low(2 * rows, width),
        low(width, 2 * rows),
        low(width, rows),
        low(HEADS, PATCH, PATCH),
        low(width, 2 * rows),
        low(total, rows),
    ]
    query, value, key_t, attn_t, probs, points_t, pick_table = call(
        forward_kernel,
        saved,
        [core, at, near_sent, far_sent, near, far, w_qkv, w_qkv[:, width:].T],
        FORWARD_FLOPS,
        [SMEM] + [VMEM] * 5 + [HBM] * 2,
        [HBM] * len(saved),
        [space(low(2 * rows, width)), space(low(width, 3 * width)), space(low(2 * width, width))]
        + [space(x) for x in saved]
        + [pltpu.SemaphoreType.DMA((12 + HEADS,))],
        60,
    )
    held = [got_grads, w_out, query, value, key_t, attn_t, points_t, w_qkv, probs]
    made = [
        low(width // 2, 4 * width),
        low(width // 2, 4 * width),
        low(rows, width),
        low(rows, 2 * width),
        low(half, width),
        low(half, width),
    ]
    send, keep, grad_query, grad_kv, near, far = call(
        backward_kernel,
        made,
        [core, at, *held],
        32 * rows * rows * width + 22 * rows * width * width,
        [SMEM, VMEM] + [HBM] * len(held),
        [HBM] * len(made),
        [space(x) for x in held]
        + [space(low(rows, width)), space(low(2 * rows, 2 * width)), space(wide(width, rows))]
        + [space(x) for x in (*made[:2], *made[4:])]
        + [pltpu.SemaphoreType.DMA((15 + HEADS,))],
        63,
    )
    kept, got = sum_core(keep, send, sides)
    near, far = halo(near, far)
    picked = low(total, width)
    picked, done = call(
        pick_kernel,
        [picked, wide(8, LANES)],
        [core, near, far, grad_query, grad_kv, w_qkv, pick_table],
        place_flops,
        [SMEM] + [HBM] * 6,
        [HBM, VMEM],
        [space(x) for x in (near, far, grad_query, grad_kv, w_qkv, pick_table, picked)] + [pltpu.SemaphoreType.DMA((10,))],
        63,
    )
    mine, sends = sum_xy(kept, got, done)
    gathered, line, n_line = sum_line(mine, sends)
    picked = gate(picked, gathered, flops=GATE_FLOPS)
    returned = exchange(picked.reshape(n_dev, cap, width)).reshape(total, width)
    weight_qkv, weight_out = sum_finish(gathered, line, n_line, sides, 3 * width)
    (result,) = call(restore_kernel, [low(rows, width)], [restore_table, returned], place_flops)
    return (result[None], weight_qkv, weight_out)


def solution(mesh):
    placed = (
        P("dp", "curve", None),
        P("dp", "curve", None),
        P("dp", "curve"),
        P("dp", "curve"),
        P(),
        P(),
    )
    return jax.shard_map(
        on_device,
        mesh=mesh,
        in_specs=placed,
        out_specs=(P("dp", "curve", None), P(), P()),
        check_vma=False,
    )
```
